32 devices in a mesh: grp: 2 (over y), dev: 8 (over z, x), layer: 2 (over core).
Axes of the slice: x: 2, y: 2, z: 4, core: 2. Of those that a mesh axis runs over, the one named last changes fastest.
Arguments:
- cols: int32 [64, 8], P('grp'), parts along dimension 0, may hold values from 0 to 32, as said below
- tiles: bfloat16 [64, 8, 128, 128], P(('grp', 'dev')), parts along dimension 0, may hold values from -0.16 to 0.5, as said below
Outputs:
- purified: bfloat16 [64, 8, 128, 128], P(('grp', 'dev')), parts along dimension 0
The draws below stay inside these ranges and needn't reach their ends.
There are 2 independent parts, one for each index of `grp`. The reference program is written for one: setup_inputs(seed, part) draws one part's arguments, and reference() takes and returns one part's arrays. A program takes and returns all parts, laid end to end along the dimension named above; each array names one. Nothing has to cross between parts.
Inputs may be any that keep to these rules, and one draw needn't show every extreme that they name: `cols`: in block row i slot 0 holds i itself; the filled slots hold distinct block columns c with (c - i) mod 32 or (i - c) mod 32 at most 4; empty slots hold 32 and come after the filled ones; a row holds 5 to 8 filled slots, and some rows are full. `tiles`: blocks in empty slots are zero.
All inputs are finite; a program needn't handle non-finite values.
Results may differ from the reference program's by a relative error of at most 0.0086.
Values may be sent and summed in bfloat16 or wider, within the bound.
No kernel may reach another device: no remote copies, remote signals or barrier semaphores. Data moves between devices by JAX's collectives and lax.ppermute only.
A program may use at most 64 MiB of HBM per device.

```python
import jax
import jax.numpy as jnp
from jax import lax

BS = 128
K = 8
ITERS = 2
NB = 32


def band_pattern(key):
    key = jax.random.fold_in(key, 17)
    order_key, count_key = jax.random.split(key)
    band_half = K // 2
    steps_up = jnp.arange(1, band_half + 1, dtype=jnp.int32)
    side = jnp.concatenate([steps_up, -steps_up])
    scores = jax.random.randint(order_key, (NB, K), 0, 1 << 20) * K + jnp.arange(K, dtype=jnp.int32)[None, :]
    picked = side[jnp.argsort(scores, axis=1)]
    offsets = jnp.concatenate([jnp.zeros((NB, 1), jnp.int32), picked[:, :K - 1]], axis=1)
    counts = jax.random.randint(count_key, (NB,), band_half + 1, K + 1)
    counts = jnp.where(jnp.arange(NB) % 5 == 0, K, counts)
    row_ids = jnp.arange(NB, dtype=jnp.int32)
    columns = (row_ids[:, None] + offsets) % NB
    filled = jnp.arange(K, dtype=jnp.int32)[None, :] < counts[:, None]
    return jnp.where(filled, columns, NB).astype(jnp.int32)


def draw_cols(key, part):
    return band_pattern(key)


def draw_tiles(key, part):
    columns = band_pattern(key)
    key = jax.random.fold_in(key, 3)
    noise_key, diag_key = jax.random.split(key)
    noise = 0.025 * jax.random.truncated_normal(noise_key, -6.0, 6.0, (NB, K, BS, BS), jnp.float32)
    levels = jax.random.uniform(diag_key, (NB, BS), jnp.float32, 0.1, 0.35)
    diagonal = levels[:, :, None] * jnp.eye(BS, dtype=jnp.float32)[None]
    first = noise[:, 0:1] + diagonal[:, None]
    blocks = jnp.concatenate([first, noise[:, 1:]], axis=1)
    blocks = jnp.where((columns < NB)[:, :, None, None], blocks, 0.0)
    return blocks.astype(jnp.bfloat16)


def setup_inputs(seed: int = 0, part: int = 0) -> dict:
    splits = jax.random.split(jax.random.key(seed), 3)
    own_keys = jax.random.split(jax.random.fold_in(splits[2], part), 3)
    return {
        "cols": draw_cols(jax.random.fold_in(jax.random.fold_in(splits[2], part), 71), part),
        "tiles": draw_tiles(jax.random.fold_in(jax.random.fold_in(splits[2], part), 71), part),
    }


def restricted_product(left, right, cols):
    total_rows = cols.shape[0]

    def one_row(row_index):
        row_cols = cols[row_index]
        partners = jnp.minimum(row_cols, total_rows - 1).astype(jnp.int32)
        partner_cols = cols[partners]
        fetched = right[partners].astype(jnp.float32)
        valid = (row_cols < total_rows)[None, :, None]
        match = ((partner_cols[:, None, :] == row_cols[None, :, None]) & valid).astype(jnp.float32)
        aligned = jnp.einsum("mnq,mqab->mnab", match, fetched)
        return jnp.einsum("mab,mnbc->nac", left[row_index].astype(jnp.float32), aligned)

    return lax.map(one_row, jnp.arange(total_rows, dtype=jnp.int32))


def reference(cols, tiles):
    current = tiles
    for iteration in range(ITERS):
        square = restricted_product(current, current, cols).astype(jnp.bfloat16)
        cube_term = restricted_product(square, current, cols)
        current = (3.0 * square.astype(jnp.float32) - 2.0 * cube_term).astype(jnp.bfloat16)
    return current
```

```python
import functools

import jax
import jax.numpy as jnp
from jax import lax
from jax.experimental import pallas as pl
from jax.experimental.pallas import tpu as pltpu
from jax.sharding import PartitionSpec as P

BS = 128
ROWS = 4
HALF = 4
FAR = 8
WINDOW = 16
TILE = 2 * BS


def start_of(row):
    return 5 * row + row * (row - 1) // 2


PACKED = start_of(ROWS)


def place(cols_ref, info_ref, index, slot):
    total = cols_ref.shape[1]
    base, sign = info_ref[0], info_ref[1]
    row = lax.rem(base + sign * (index - FAR) + total, total)
    column = cols_ref[slot, row]
    where = lax.rem(sign * (column - base) + FAR + 2 * total, total)
    return where, (column < total) & (where < WINDOW)


def local_row(info_ref, row):
    return jnp.where(info_ref[1] > 0, row, ROWS - 1 - row)


def block(index, first=0):
    return pl.ds((index - first) * BS, BS)


def pair(index, first=0, count=1):
    return pl.ds((2 * index - first) * BS, count * TILE)


def lanes(index, first=0):
    return pl.ds(pl.multiple_of((index - first) * BS, BS), BS)


def pack_kernel(cols_ref, info_ref, tiles_ref, out_ref):
    out_ref[...] = jnp.zeros_like(out_ref)
    slots = cols_ref.shape[0]
    for row in range(ROWS):
        held = local_row(info_ref, row)
        for slot in range(slots):
            where, filled = place(cols_ref, info_ref, FAR + row, slot)

            @pl.when(filled & (where >= FAR))
            def _():
                out_ref[start_of(row) + where - FAR] = tiles_ref[held, slot]


def spread(cols_ref, info_ref, source_ref, index, target_ref, first_row, first_column, mask_ref=None):
    slots = cols_ref.shape[0]
    for row in range(ROWS):
        held = local_row(info_ref, row)
        for slot in range(slots):
            where, filled = place(cols_ref, info_ref, index + row, slot)

            @pl.when(filled & (where >= first_column))
            def _():
                target_ref[block(index + row, first_row), lanes(where, first_column)] = source_ref[held, slot]


def mark(cols_ref, info_ref, index, mask_ref):
    slots = cols_ref.shape[0]
    for row in range(ROWS):
        for column in range(WINDOW):
            mask_ref[row, column] = 0
        for slot in range(slots):
            where, filled = place(cols_ref, info_ref, index + row, slot)

            @pl.when(filled)
            def _():
                mask_ref[row, where] = 1


def kept(value, mask_ref, row, column):
    parts = []
    for down in range(2):
        across = []
        for right in range(2):
            one = value[down * BS:(down + 1) * BS, right * BS:(right + 1) * BS]
            across.append(jnp.where(mask_ref[row + down, column + right] > 0, one, jnp.zeros_like(one)))
        parts.append(jnp.concatenate(across, axis=1))
    return jnp.concatenate(parts, axis=0)


def product(left, right, row_pair, column_pair, low, high):
    start = max(row_pair - 2, column_pair - 2, low)
    stop = min(row_pair + 2, column_pair + 2, high) + 1
    total = None
    while start < stop:
        end, a, b = start + 1, left(row_pair, start), right(start, column_pair)
        while end < stop:
            a2, b2 = left(row_pair, end), right(end, column_pair)
            if a2[0] is not a[0] or b2[0] is not b[0]:
                break
            end += 1
        count = (end - start) * TILE
        part = jnp.dot(
            a[0][pl.ds(a[1], TILE), pl.ds(a[2], count)],
            b[0][pl.ds(b[1], count), pl.ds(b[2], TILE)],
            preferred_element_type=jnp.float32,
        )
        total = part if total is None else total + part
        start = end
    return total


def view(ref, first_row, first_column):
    return lambda row_pair, column_pair: (
        ref, (2 * row_pair - first_row) * BS, (2 * column_pair - first_column) * BS
    )


def purify(left, right, square_ref, square, mask_ref, first_row, pairs, low, high, column_pairs, write):
    for row_pair in pairs:
        row = 2 * row_pair - first_row
        for column_pair in range(max(row_pair - 2, low), min(row_pair + 2, high) + 1):
            value = product(left, right, row_pair, column_pair, low, high)
            _, r, c = square(row_pair, column_pair)
            square_ref[pl.ds(r, TILE), pl.ds(c, TILE)] = kept(
                value, mask_ref, row, 2 * column_pair
            ).astype(jnp.bfloat16)
    for row_pair in pairs:
        row = 2 * row_pair - first_row
        for column_pair in column_pairs(row_pair):
            cube = product(square, right, row_pair, column_pair, low, high)
            _, r, c = square(row_pair, column_pair)
            own = square_ref[pl.ds(r, TILE), pl.ds(c, TILE)].astype(jnp.float32)
            value = 3.0 * own - 2.0 * kept(cube, mask_ref, row, 2 * column_pair)
            write(row_pair, column_pair, value.astype(jnp.bfloat16))


def own_kernel(cols_ref, info_ref, tiles_ref, near_ref, other_ref, low_ref, own_ref, next_ref, high_ref, square_ref, mask_ref):
    low_ref[...] = jnp.zeros_like(low_ref)
    own_ref[...] = jnp.zeros_like(own_ref)
    high_ref[...] = jnp.zeros_like(high_ref)
    spread(cols_ref, info_ref, near_ref, 4, low_ref, 4, 0)
    spread(cols_ref, info_ref, tiles_ref, 8, own_ref, 8, 4)
    spread(cols_ref, info_ref, other_ref, 12, high_ref, 12, 8)
    mark(cols_ref, info_ref, 8, mask_ref)
    views = {2: view(low_ref, 4, 0), 4: view(own_ref, 8, 4), 6: view(high_ref, 12, 8)}

    def right(row_pair, column_pair):
        return views[row_pair // 2 * 2](row_pair, column_pair)

    square = view(square_ref, 8, 4)

    def write(row_pair, column_pair, value):
        next_ref[pair(row_pair, 8), pair(column_pair, 4)] = value

    next_ref[...] = jnp.zeros_like(next_ref)
    purify(
        view(own_ref, 8, 4), right, square_ref, square, mask_ref, 8, (4, 5), 2, 7,
        lambda p: range(p - 2, p + 3), write,
    )


def far_kernel(cols_ref, info_ref, far_ref, low_ref, own_ref, next_ref, dense_ref, square_ref, mask_ref):
    for row in range(ROWS):
        for column in range(8):
            if column < row + 5:
                dense_ref[block(row), block(column)] = far_ref[start_of(row) + column]
            else:
                dense_ref[block(row), block(column)] = jnp.zeros((BS, BS), jnp.bfloat16)
    mark(cols_ref, info_ref, 4, mask_ref)
    views = {0: view(dense_ref, 0, 0), 2: view(low_ref, 4, 0), 4: view(own_ref, 8, 4)}

    def right(row_pair, column_pair):
        return views[row_pair // 2 * 2](row_pair, column_pair)

    def write(row_pair, column_pair, value):
        next_ref[pair(row_pair, 4), pair(column_pair, 4)] = value

    next_ref[pl.ds(0, TILE), pl.ds(3 * TILE, TILE)] = jnp.zeros((TILE, TILE), jnp.bfloat16)
    purify(
        view(low_ref, 4, 0), right, square_ref, view(square_ref, 4, 0), mask_ref, 4, (2, 3), 0, 5,
        lambda p: range(2, p + 3), write,
    )


def last_kernel(cols_ref, info_ref, low_ref, own_ref, other_ref, out_ref, high_ref, square_ref, mask_ref, dense_ref):
    for row in range(ROWS):
        for column in range(8):
            high_ref[block(3 - row), block(7 - column)] = other_ref[block(row), block(column)]
    mark(cols_ref, info_ref, 8, mask_ref)
    views = {2: view(low_ref, 4, 4), 4: view(own_ref, 8, 4), 6: view(high_ref, 12, 8)}

    def right(row_pair, column_pair):
        return views[row_pair // 2 * 2](row_pair, column_pair)

    def write(row_pair, column_pair, value):
        dense_ref[pair(row_pair, 8), pair(column_pair, 4)] = value

    purify(
        view(own_ref, 8, 4), right, square_ref, view(square_ref, 8, 4), mask_ref, 8, (4, 5), 2, 7,
        lambda p: range(p - 2, p + 3), write,
    )
    slots = cols_ref.shape[0]
    for row in range(ROWS):
        held = local_row(info_ref, row)
        for slot in range(slots):
            where, filled = place(cols_ref, info_ref, FAR + row, slot)

            @pl.when(filled)
            def _():
                out_ref[held, slot] = dense_ref[block(row), lanes(where, 4)]

            @pl.when(jnp.logical_not(filled))
            def _():
                out_ref[held, slot] = jnp.zeros((BS, BS), jnp.bfloat16)


def call(kernel, operands, outs, scratch, name, flops=0):
    smem, vmem = pl.BlockSpec(memory_space=pltpu.SMEM), pl.BlockSpec(memory_space=pltpu.VMEM)
    shapes = [jax.ShapeDtypeStruct(shape, jnp.bfloat16) for shape in outs]
    moved = sum(2 * x.size for x in operands[2:]) + sum(2 * s.size for s in shapes)
    return pl.pallas_call(
        kernel,
        out_shape=shapes,
        in_specs=[smem, smem] + [vmem] * (len(operands) - 2),
        out_specs=[vmem] * len(shapes),
        scratch_shapes=scratch,
        compiler_params=pltpu.CompilerParams(vmem_limit_bytes=40 * 2**20),
        cost_estimate=pl.CostEstimate(flops=flops, bytes_accessed=moved, transcendentals=0),
        name=name,
    )(*operands)


def per_device(cols, tiles):
    devices = lax.axis_size("dev")
    first = lax.axis_index("dev") * ROWS
    layer = lax.axis_index("layer")
    info = jnp.stack([first + layer * (ROWS - 1), 1 - 2 * layer]).astype(jnp.int32)
    cols = cols.T
    axes = ("dev", "layer")

    def shifted(value, step):
        pairs = []
        for i in range(devices):
            pairs.append((2 * i, (i + step) % devices * 2))
            pairs.append((2 * i + 1, (i - step) % devices * 2 + 1))
        return lax.ppermute(value, axes, pairs)

    def swapped(value):
        return lax.ppermute(value, "layer", [(0, 1), (1, 0)])

    bf16 = jnp.bfloat16
    mask = pltpu.SMEM((ROWS, WINDOW), jnp.int32)
    near = shifted(tiles, 1)
    (packed,) = call(pack_kernel, (cols, info, tiles), [(PACKED, BS, BS)], [], "pack")
    far = shifted(packed, 2)
    other = swapped(near)
    unit = 2 * TILE**3
    low, own, current = call(
        own_kernel, (cols, info, tiles, near, other),
        [(ROWS * BS, 12 * BS), (ROWS * BS, 12 * BS), (ROWS * BS, 12 * BS)],
        [pltpu.VMEM((ROWS * BS, 8 * BS), bf16), pltpu.VMEM((ROWS * BS, 12 * BS), bf16), mask],
        "own", 76 * unit,
    )
    (current_low,) = call(
        far_kernel, (cols, info, far, low, own),
        [(ROWS * BS, 8 * BS)],
        [pltpu.VMEM((ROWS * BS, 8 * BS), bf16), pltpu.VMEM((ROWS * BS, 12 * BS), bf16), mask],
        "far", 66 * unit,
    )
    current_other = swapped(current_low)
    (out,) = call(
        last_kernel, (cols, info, current_low, current, current_other),
        [tiles.shape],
        [pltpu.VMEM((ROWS * BS, 8 * BS), bf16), pltpu.VMEM((ROWS * BS, 12 * BS), bf16), mask,
         pltpu.VMEM((ROWS * BS, 12 * BS), bf16)],
        "last", 76 * unit,
    )
    return out


def solution(mesh):
    return jax.shard_map(
        per_device,
        mesh=mesh,
        in_specs=(P("grp", None), P(("grp", "dev"), None, None, None)),
        out_specs=P(("grp", "dev"), None, None, None),
        check_vma=False,
    )
```

```python
import functools

import jax
import jax.numpy as jnp
from jax import lax
from jax.experimental import pallas as pl
from jax.experimental.pallas import tpu as pltpu
from jax.sharding import PartitionSpec as P

BS = 128
ROWS = 4
HALF = 4
FAR = 8
WINDOW = 16
TILE = 2 * BS


def start_of(row):
    return 5 * row + row * (row - 1) // 2


PACKED = start_of(ROWS)


def place(cols_ref, info_ref, index, slot):
    total = cols_ref.shape[1]
    base, sign = info_ref[0], info_ref[1]
    row = lax.rem(base + sign * (index - FAR) + total, total)
    column = cols_ref[slot, row]
    where = lax.rem(sign * (column - base) + FAR + 2 * total, total)
    return where, (column < total) & (where < WINDOW)


def local_row(info_ref, row):
    return jnp.where(info_ref[1] > 0, row, ROWS - 1 - row)


def block(index, first=0):
    return pl.ds((index - first) * BS, BS)


def pair(index, first=0, count=1):
    return pl.ds((2 * index - first) * BS, count * TILE)


def lanes(index, first=0):
    return pl.ds(pl.multiple_of((index - first) * BS, BS), BS)


def pack_kernel(cols_ref, info_ref, tiles_ref, out_ref):
    out_ref[...] = jnp.zeros_like(out_ref)
    slots = cols_ref.shape[0]
    for row in range(ROWS):
        held = local_row(info_ref, row)
        for slot in range(slots):
            where, filled = place(cols_ref, info_ref, FAR + row, slot)

            @pl.when(filled & (where >= FAR))
            def _():
                out_ref[start_of(row) + where - FAR] = tiles_ref[held, slot]


def spread(cols_ref, info_ref, fetch, index, target_ref, first_row, first_column):
    slots = cols_ref.shape[0]
    for row in range(ROWS):
        held = local_row(info_ref, row)
        for slot in range(slots):
            where, filled = place(cols_ref, info_ref, index + row, slot)

            @pl.when(filled & (where >= first_column))
            def _():
                target_ref[block(index + row, first_row), lanes(where, first_column)] = fetch(held, slot)


def mark(cols_ref, info_ref, index, mask_ref):
    slots = cols_ref.shape[0]
    for row in range(ROWS):
        for column in range(WINDOW):
            mask_ref[row, column] = 0
        for slot in range(slots):
            where, filled = place(cols_ref, info_ref, index + row, slot)

            @pl.when(filled)
            def _():
                mask_ref[row, where] = 1


def kept(value, mask_ref, row, column):
    parts = []
    for down in range(2):
        across = []
        for right in range(2):
            one = value[down * BS:(down + 1) * BS, right * BS:(right + 1) * BS]
            across.append(jnp.where(mask_ref[row + down, column + right] > 0, one, jnp.zeros_like(one)))
        parts.append(jnp.concatenate(across, axis=1))
    return jnp.concatenate(parts, axis=0)


def product(left, right, row_pair, column_pair, low, high):
    start = max(row_pair - 2, column_pair - 2, low)
    stop = min(row_pair + 2, column_pair + 2, high) + 1
    total = None
    while start < stop:
        end, a, b = start + 1, left(row_pair, start), right(start, column_pair)
        while end < stop:
            a2, b2 = left(row_pair, end), right(end, column_pair)
            if a2[0] is not a[0] or b2[0] is not b[0]:
                break
            end += 1
        count = (end - start) * TILE
        part = jnp.dot(
            a[0][pl.ds(a[1], TILE), pl.ds(a[2], count)],
            b[0][pl.ds(b[1], count), pl.ds(b[2], TILE)],
            preferred_element_type=jnp.float32,
        )
        total = part if total is None else total + part
        start = end
    return total


def view(ref, first_row, first_column):
    return lambda row_pair, column_pair: (
        ref, (2 * row_pair - first_row) * BS, (2 * column_pair - first_column) * BS
    )


def purify(left, right, square_ref, square, mask_ref, first_row, pairs, low, high, column_pairs, write):
    for row_pair in pairs:
        row = 2 * row_pair - first_row
        for column_pair in range(max(row_pair - 2, low), min(row_pair + 2, high) + 1):
            value = product(left, right, row_pair, column_pair, low, high)
            _, r, c = square(row_pair, column_pair)
            square_ref[pl.ds(r, TILE), pl.ds(c, TILE)] = kept(
                value, mask_ref, row, 2 * column_pair
            ).astype(jnp.bfloat16)
    for row_pair in pairs:
        row = 2 * row_pair - first_row
        for column_pair in column_pairs(row_pair):
            cube = product(square, right, row_pair, column_pair, low, high)
            _, r, c = square(row_pair, column_pair)
            own = square_ref[pl.ds(r, TILE), pl.ds(c, TILE)].astype(jnp.float32)
            value = 3.0 * own - 2.0 * kept(cube, mask_ref, row, 2 * column_pair)
            write(row_pair, column_pair, value.astype(jnp.bfloat16))


def own_kernel(cols_ref, info_ref, tiles_ref, near_ref, other0_ref, other1_ref, low_ref, own_ref, next_ref, high_ref, square_ref, mask_ref):
    low_ref[...] = jnp.zeros_like(low_ref)
    own_ref[...] = jnp.zeros_like(own_ref)
    high_ref[...] = jnp.zeros_like(high_ref)
    spread(cols_ref, info_ref, lambda row, slot: near_ref[row, slot], 4, low_ref, 4, 0)
    spread(cols_ref, info_ref, lambda row, slot: tiles_ref[row, slot], 8, own_ref, 8, 4)
    spread(
        cols_ref, info_ref,
        lambda row, slot: jnp.where(row < 2, other0_ref[row % 2, slot], other1_ref[row % 2, slot]),
        12, high_ref, 12, 8,
    )
    mark(cols_ref, info_ref, 8, mask_ref)
    views = {2: view(low_ref, 4, 0), 4: view(own_ref, 8, 4), 6: view(high_ref, 12, 8)}

    def right(row_pair, column_pair):
        return views[row_pair // 2 * 2](row_pair, column_pair)

    square = view(square_ref, 8, 4)

    def write(row_pair, column_pair, value):
        next_ref[pair(row_pair, 8), pair(column_pair, 4)] = value

    next_ref[...] = jnp.zeros_like(next_ref)
    purify(
        view(own_ref, 8, 4), right, square_ref, square, mask_ref, 8, (4, 5), 2, 7,
        lambda p: range(p - 2, p + 3), write,
    )


def far_kernel(cols_ref, info_ref, far_ref, low_ref, own_ref, next_ref, dense_ref, square_ref, mask_ref):
    for row in range(ROWS):
        for column in range(8):
            if column < row + 5:
                dense_ref[block(row), block(column)] = far_ref[start_of(row) + column]
            else:
                dense_ref[block(row), block(column)] = jnp.zeros((BS, BS), jnp.bfloat16)
    mark(cols_ref, info_ref, 4, mask_ref)
    views = {0: view(dense_ref, 0, 0), 2: view(low_ref, 4, 0), 4: view(own_ref, 8, 4)}

    def right(row_pair, column_pair):
        return views[row_pair // 2 * 2](row_pair, column_pair)

    def write(row_pair, column_pair, value):
        next_ref[pair(row_pair, 4), pair(column_pair, 4)] = value

    next_ref[pl.ds(0, TILE), pl.ds(3 * TILE, TILE)] = jnp.zeros((TILE, TILE), jnp.bfloat16)
    purify(
        view(low_ref, 4, 0), right, square_ref, view(square_ref, 4, 0), mask_ref, 4, (2, 3), 0, 5,
        lambda p: range(2, p + 3), write,
    )


def last_kernel(cols_ref, info_ref, low_ref, own_ref, other_ref, out_ref, high_ref, square_ref, mask_ref, dense_ref):
    for row in range(ROWS):
        for column in range(8):
            high_ref[block(3 - row), block(7 - column)] = other_ref[block(row), block(column)]
    mark(cols_ref, info_ref, 8, mask_ref)
    views = {2: view(low_ref, 4, 4), 4: view(own_ref, 8, 4), 6: view(high_ref, 12, 8)}

    def right(row_pair, column_pair):
        return views[row_pair // 2 * 2](row_pair, column_pair)

    def write(row_pair, column_pair, value):
        dense_ref[pair(row_pair, 8), pair(column_pair, 4)] = value

    purify(
        view(own_ref, 8, 4), right, square_ref, view(square_ref, 8, 4), mask_ref, 8, (4, 5), 2, 7,
        lambda p: range(p - 2, p + 3), write,
    )
    slots = cols_ref.shape[0]
    for row in range(ROWS):
        held = local_row(info_ref, row)
        for slot in range(slots):
            where, filled = place(cols_ref, info_ref, FAR + row, slot)

            @pl.when(filled)
            def _():
                out_ref[held, slot] = dense_ref[block(row), lanes(where, 4)]

            @pl.when(jnp.logical_not(filled))
            def _():
                out_ref[held, slot] = jnp.zeros((BS, BS), jnp.bfloat16)


def call(kernel, operands, outs, scratch, name, flops=0):
    smem, vmem = pl.BlockSpec(memory_space=pltpu.SMEM), pl.BlockSpec(memory_space=pltpu.VMEM)
    shapes = [jax.ShapeDtypeStruct(shape, jnp.bfloat16) for shape in outs]
    moved = sum(2 * x.size for x in operands[2:]) + sum(2 * s.size for s in shapes)
    return pl.pallas_call(
        kernel,
        out_shape=shapes,
        in_specs=[smem, smem] + [vmem] * (len(operands) - 2),
        out_specs=[vmem] * len(shapes),
        scratch_shapes=scratch,
        compiler_params=pltpu.CompilerParams(vmem_limit_bytes=40 * 2**20),
        cost_estimate=pl.CostEstimate(flops=flops, bytes_accessed=moved, transcendentals=0),
        name=name,
    )(*operands)


def per_device(cols, tiles):
    devices = lax.axis_size("dev")
    first = lax.axis_index("dev") * ROWS
    layer = lax.axis_index("layer")
    info = jnp.stack([first + layer * (ROWS - 1), 1 - 2 * layer]).astype(jnp.int32)
    cols = cols.T
    axes = ("dev", "layer")

    def shifted(value, step):
        pairs = []
        for i in range(devices):
            pairs.append((2 * i, (i + step) % devices * 2))
            pairs.append((2 * i + 1, (i - step) % devices * 2 + 1))
        return lax.ppermute(value, axes, pairs)

    def swapped(value):
        return lax.ppermute(value, "layer", [(0, 1), (1, 0)])

    bf16 = jnp.bfloat16
    mask = pltpu.SMEM((ROWS, WINDOW), jnp.int32)
    near = shifted(tiles, 1)
    (packed,) = call(pack_kernel, (cols, info, tiles), [(PACKED, BS, BS)], [], "pack")
    far = shifted(packed, 2)
    near, packed = lax.optimization_barrier((near, packed))
    other = [swapped(near[:2]), swapped(near[2:])]
    unit = 2 * TILE**3
    low, own, current = call(
        own_kernel, (cols, info, tiles, near, *other),
        [(ROWS * BS, 12 * BS), (ROWS * BS, 12 * BS), (ROWS * BS, 12 * BS)],
        [pltpu.VMEM((ROWS * BS, 8 * BS), bf16), pltpu.VMEM((ROWS * BS, 12 * BS), bf16), mask],
        "own", 76 * unit,
    )
    (current_low,) = call(
        far_kernel, (cols, info, far, low, own),
        [(ROWS * BS, 8 * BS)],
        [pltpu.VMEM((ROWS * BS, 8 * BS), bf16), pltpu.VMEM((ROWS * BS, 12 * BS), bf16), mask],
        "far", 66 * unit,
    )
    current_other = swapped(current_low)
    (out,) = call(
        last_kernel, (cols, info, current_low, current, current_other),
        [tiles.shape],
        [pltpu.VMEM((ROWS * BS, 8 * BS), bf16), pltpu.VMEM((ROWS * BS, 12 * BS), bf16), mask,
         pltpu.VMEM((ROWS * BS, 12 * BS), bf16)],
        "last", 76 * unit,
    )
    return out


def solution(mesh):
    return jax.shard_map(
        per_device,
        mesh=mesh,
        in_specs=(P("grp", None), P(("grp", "dev"), None, None, None)),
        out_specs=P(("grp", "dev"), None, None, None),
        check_vma=False,
    )
```

```python
import functools

import jax
import jax.numpy as jnp
from jax import lax
from jax.experimental import pallas as pl
from jax.experimental.pallas import tpu as pltpu
from jax.sharding import PartitionSpec as P

BS = 128
ROWS = 4
HALF = 4
FAR = 8
WINDOW = 16
TILE = 2 * BS


def start_of(row):
    return 5 * row + row * (row - 1) // 2


PACKED = start_of(ROWS)
SLOTS = 2 * HALF


def block(index, first=0):
    return pl.ds((index - first) * BS, BS)


def lanes(index, first=0):
    return pl.ds(pl.multiple_of((index - first) * BS, BS), BS)


def tile(index, first=0):
    return pl.ds((2 * index - first) * BS, TILE)


def local_row(info_ref, row):
    return jnp.where(info_ref[1] > 0, row, ROWS - 1 - row)


def pack_kernel(info_ref, cols_ref, tiles_ref, out_ref, table_ref, sem):
    total = cols_ref.shape[1]
    table = pltpu.make_async_copy(cols_ref, table_ref, sem)
    table.start()
    out_ref[...] = jnp.zeros_like(out_ref)
    table.wait()
    base, sign = info_ref[0], info_ref[1]
    copies = []
    for row in range(ROWS):
        held = local_row(info_ref, row)
        for slot in range(SLOTS):
            column = table_ref[slot, base + sign * row]
            where = lax.rem(sign * (column - base) + total, total)
            wanted = (column < total) & (where < HALF + ROWS)
            target = jnp.where(wanted, start_of(row) + where, 0)
            copy = pltpu.make_async_copy(tiles_ref.at[held, slot], out_ref.at[target], sem)
            copies.append((wanted, copy))
            pl.when(wanted)(copy.start)
    for wanted, copy in copies:
        pl.when(wanted)(copy.wait)


def spread(info_ref, place_ref, sources, index, target_ref, first_column):
    last = target_ref.shape[1] // BS - 1
    count = ROWS // len(sources)
    for row in range(ROWS):
        held = local_row(info_ref, row)
        for slot in range(SLOTS):
            where = jnp.minimum(place_ref[(index + row) * SLOTS + slot] - first_column, last)
            value = sources[0][held % count, slot]
            for i in range(1, len(sources)):
                value = jnp.where(held >= i * count, sources[i][held % count, slot], value)
            target_ref[block(row), lanes(where)] = value


def kept(value, mask_ref, row_pair, column_pair):
    parts = []
    for down in range(2):
        across = []
        for right in range(2):
            one = value[down * BS:(down + 1) * BS, right * BS:(right + 1) * BS]
            there = mask_ref[(2 * row_pair + down) * WINDOW + 2 * column_pair + right] > 0
            across.append(jnp.where(there, one, jnp.zeros_like(one)))
        parts.append(jnp.concatenate(across, axis=1))
    return jnp.concatenate(parts, axis=0)


class Dense:
    def __init__(self, ref, first_row, first_column):
        self.ref, self.first_row, self.first_column = ref, first_row, first_column

    def rows(self, row_pair, count=1):
        return pl.ds((2 * row_pair - self.first_row) * BS, count * TILE)

    def columns(self, column_pair, count=1):
        return pl.ds((2 * column_pair - self.first_column) * BS, count * TILE)

    def __getitem__(self, at):
        return self.ref[self.rows(at[0]), self.columns(at[1])]

    def __setitem__(self, at, value):
        self.ref[self.rows(at[0]), self.columns(at[1])] = value


def product(left, right, row_pair, column_pair, ks):
    ks = [k for k in sorted(ks) if abs(k - row_pair) <= 2 and abs(k - column_pair) <= 2]
    total = None
    while ks:
        source = right[ks[0]]
        count = 1
        while count < len(ks) and ks[count] == ks[0] + count and right[ks[count]].ref is source.ref:
            count += 1
        part = jnp.dot(
            left.ref[left.rows(row_pair), left.columns(ks[0], count)],
            source.ref[source.rows(ks[0], count), source.columns(column_pair)],
            preferred_element_type=jnp.float32,
        )
        total = part if total is None else total + part
        ks = ks[count:]
    return total


class Step:
    def __init__(self, pairs, low, high, early, late, wanted):
        self.pairs, self.low, self.high, self.early, self.late, self.wanted = pairs, low, high, early, late, wanted

    def columns(self, row_pair):
        return range(max(row_pair - 2, self.low), min(row_pair + 2, self.high) + 1)

    def whole(self, row_pair, column_pair):
        return not any(abs(k - row_pair) <= 2 and abs(k - column_pair) <= 2 for k in self.late)

    def open(self):
        squares = [(p, c) for p in self.pairs for c in self.columns(p) if not self.whole(p, c)]
        cubes = [(p, c) for p in self.pairs for c in self.wanted(p) if self.done(p, c)]
        return {at: i for i, at in enumerate(squares)}, {at: i for i, at in enumerate(cubes)}

    def done(self, row_pair, column_pair):
        return [k for k in self.columns(row_pair) if self.whole(row_pair, k) and abs(k - column_pair) <= 2]

    def first(self, left, right, square, mask_ref, square_part, cube_part):
        squares, cubes = self.open()
        for p in self.pairs:
            for c in self.columns(p):
                value = product(left, right, p, c, self.early)
                if (p, c) in squares:
                    square_part[squares[p, c]] = value
                else:
                    square[p, c] = kept(value, mask_ref, p, c).astype(jnp.bfloat16)
        for (p, c), i in cubes.items():
            cube_part[i] = product(square, right, p, c, self.done(p, c))

    def second(self, left, right, square, ready, mask_ref, square_part, cube_part, write):
        squares, cubes = self.open()
        for (p, c), i in squares.items():
            value = square_part[i] + product(left, right, p, c, self.late)
            square[p, c] = kept(value, mask_ref, p, c).astype(jnp.bfloat16)
        for p in self.pairs:
            for c in self.wanted(p):
                rest = [k for k in self.columns(p) if not self.whole(p, k)]
                cube = product(square, right, p, c, rest)
                if (p, c) in cubes:
                    cube = cube_part[cubes[p, c]] if cube is None else cube_part[cubes[p, c]] + cube
                own = (square if (p, c) in squares else ready)[p, c].astype(jnp.float32)
                write(p, c, (3.0 * own - 2.0 * kept(cube, mask_ref, p, c)).astype(jnp.bfloat16))

    def all(self, left, right, square, mask_ref, write):
        for p in self.pairs:
            for c in self.columns(p):
                value = product(left, right, p, c, self.early)
                square[p, c] = kept(value, mask_ref, p, c).astype(jnp.bfloat16)
        for p in self.pairs:
            for c in self.wanted(p):
                cube = product(square, right, p, c, self.early)
                own = square[p, c].astype(jnp.float32)
                write(p, c, (3.0 * own - 2.0 * kept(cube, mask_ref, p, c)).astype(jnp.bfloat16))


OWN = Step((4, 5), 2, 7, (2, 3, 4, 5, 6, 7), (), lambda p: range(p - 2, p + 3))
LOW = Step((2, 3), 0, 5, (2, 3, 4, 5), (0, 1), lambda p: range(2, p + 3))
LAST = Step((4, 5), 2, 7, (2, 3, 4, 5), (6, 7), lambda p: range(p - 2, p + 3))


def own_rows_kernel(info_ref, place_ref, tiles_ref, own_ref):
    own_ref[...] = jnp.zeros_like(own_ref)
    spread(info_ref, place_ref, (tiles_ref,), 8, own_ref, 4)


def low_first_kernel(info_ref, place_ref, mask_ref, near_ref, own_ref, low_ref, square_ref, square_part, cube_part):
    low_ref[...] = jnp.zeros_like(low_ref)
    spread(info_ref, place_ref, (near_ref,), 4, low_ref, 0)
    low, own = Dense(low_ref, 4, 0), Dense(own_ref, 8, 4)
    LOW.first(low, {2: low, 3: low, 4: own, 5: own}, Dense(square_ref, 4, 8), mask_ref, square_part, cube_part)


def own_kernel(info_ref, place_ref, mask_ref, low_ref, own_ref, other0_ref, other1_ref, next_ref, high_ref, square_ref):
    high_ref[...] = jnp.zeros_like(high_ref)
    spread(info_ref, place_ref, (other0_ref, other1_ref), 12, high_ref, 8)
    low, own, high = Dense(low_ref, 4, 0), Dense(own_ref, 8, 4), Dense(high_ref, 12, 8)
    result = Dense(next_ref, 8, 4)
    next_ref[tile(4, 8), tile(7, 4)] = jnp.zeros((TILE, TILE), jnp.bfloat16)
    next_ref[tile(5, 8), tile(2, 4)] = jnp.zeros((TILE, TILE), jnp.bfloat16)

    def write(p, c, value):
        result[p, c] = value

    OWN.all(own, {2: low, 3: low, 4: own, 5: own, 6: high, 7: high}, Dense(square_ref, 8, 4), mask_ref, write)


def low_second_kernel(mask_ref, far_ref, low_ref, ready_ref, square_part, cube_part, next_ref, sent_ref, far_dense_ref, square_ref):
    for row in range(ROWS):
        for column in range(8):
            if column < row + 5:
                far_dense_ref[block(row), block(column)] = far_ref[start_of(row) + column]
            else:
                far_dense_ref[block(row), block(column)] = jnp.zeros((BS, BS), jnp.bfloat16)
    low, far = Dense(low_ref, 4, 0), Dense(far_dense_ref, 0, 0)
    result = Dense(next_ref, 4, 4)
    next_ref[tile(2, 4), tile(5, 4)] = jnp.zeros((TILE, TILE), jnp.bfloat16)

    def write(p, c, value):
        result[p, c] = value
        for down in range(2):
            for right in range(2):
                row, column = 2 * p + down - 4, 2 * c + right - 4
                if column < row + 5:
                    sent_ref[start_of(row) + column] = value[down * BS:(down + 1) * BS, right * BS:(right + 1) * BS]

    LOW.second(
        low, {0: far, 1: far, 2: low, 3: low}, Dense(square_ref, 4, 0), Dense(ready_ref, 4, 8), mask_ref,
        square_part, cube_part, write,
    )


def last_first_kernel(mask_ref, low_ref, own_ref, square_ref, square_part, cube_part):
    low, own = Dense(low_ref, 4, 4), Dense(own_ref, 8, 4)
    LAST.first(own, {2: low, 3: low, 4: own, 5: own}, Dense(square_ref, 8, 4), mask_ref, square_part, cube_part)


def last_second_kernel(info_ref, place_ref, mask_ref, own_ref, other_ref, ready_ref, square_part, cube_part,
                       out_ref, high_ref, square_ref, dense_ref):
    for row in range(ROWS):
        for column in range(8):
            if column < row + 5:
                high_ref[block(3 - row), block(7 - column)] = other_ref[start_of(row) + column]
            else:
                high_ref[block(3 - row), block(7 - column)] = jnp.zeros((BS, BS), jnp.bfloat16)
    own, high = Dense(own_ref, 8, 4), Dense(high_ref, 12, 8)
    result = Dense(dense_ref, 8, 4)
    empty = dense_ref.shape[1] // BS - 1
    dense_ref[:, block(empty)] = jnp.zeros((ROWS * BS, BS), jnp.bfloat16)

    def write(p, c, value):
        result[p, c] = value

    LAST.second(
        own, {4: own, 5: own, 6: high, 7: high}, Dense(square_ref, 8, 4), Dense(ready_ref, 8, 4), mask_ref,
        square_part, cube_part, write,
    )
    for row in range(ROWS):
        held = local_row(info_ref, row)
        for slot in range(SLOTS):
            where = place_ref[(8 + row) * SLOTS + slot] - 4
            out_ref[held, slot] = dense_ref[block(row), lanes(jnp.minimum(where, empty))]


def call(kernel, scalars, operands, outs, scratch, name, space=pltpu.VMEM, limit=12):
    smem, vmem = pl.BlockSpec(memory_space=pltpu.SMEM), pl.BlockSpec(memory_space=pltpu.VMEM)
    return pl.pallas_call(
        kernel,
        out_shape=outs,
        in_specs=[smem] * len(scalars) + [pl.BlockSpec(memory_space=space)] * len(operands),
        out_specs=[vmem] * len(outs),
        scratch_shapes=scratch,
        compiler_params=pltpu.CompilerParams(vmem_limit_bytes=limit * 2**20),
        cost_estimate=pl.CostEstimate(flops=0, bytes_accessed=0, transcendentals=0),
        name=name,
    )(*scalars, *operands)


def dense(columns, rows=ROWS):
    return jax.ShapeDtypeStruct((rows * BS, columns * BS), jnp.bfloat16)


def partial_sums(step):
    return [jax.ShapeDtypeStruct((len(part), TILE, TILE), jnp.float32) for part in step.open()]


def scratch(columns, rows=ROWS):
    return pltpu.VMEM((rows * BS, columns * BS), jnp.bfloat16)


def per_device(cols, tiles):
    devices = lax.axis_size("dev")
    total = cols.shape[0]
    layer = lax.axis_index("layer")
    base = lax.axis_index("dev") * ROWS + layer * (ROWS - 1)
    sign = 1 - 2 * layer
    info = jnp.stack([base, sign]).astype(jnp.int32)
    axes = ("dev", "layer")

    def shifted(value, step):
        pairs = []
        for i in range(devices):
            pairs.append((2 * i, (i + step) % devices * 2))
            pairs.append((2 * i + 1, (i - step) % devices * 2 + 1))
        return lax.ppermute(value, axes, pairs)

    def swapped(value):
        return lax.ppermute(value, "layer", [(0, 1), (1, 0)])

    near = shifted(tiles, 1)
    packed = jax.ShapeDtypeStruct((PACKED, BS, BS), jnp.bfloat16)
    (packed_rows,) = call(
        pack_kernel, (info,), (cols.T, tiles), [packed],
        [pltpu.SMEM(cols.T.shape, jnp.int32), pltpu.SemaphoreType.DMA], "pack", pltpu.HBM, 56,
    )
    far = shifted(packed_rows, 2)
    rows = (base + sign * (jnp.arange(WINDOW, dtype=jnp.int32) - FAR) + total) % total
    window = jnp.take(cols, rows, axis=0)
    where = (sign * (window - base) + FAR + 2 * total) % total
    where = jnp.where((window < total) & (where < WINDOW), where, WINDOW)
    place = where.reshape(-1)
    pattern = jnp.any(where[:, :, None] == jnp.arange(WINDOW, dtype=jnp.int32), axis=1)
    mask = pattern.astype(jnp.int32).reshape(-1)

    (own,) = call(own_rows_kernel, (info, place), (tiles,), [dense(13)], [], "own_rows")

    near, packed_rows, own, mask = lax.optimization_barrier((near, packed_rows, own, mask))
    other = [swapped(near[:2]), swapped(near[2:])]
    low, ready, *parts = call(
        low_first_kernel, (info, place, mask), (near, own), [dense(13), dense(4), *partial_sums(LOW)], [], "low_first"
    )
    (current,) = call(
        own_kernel, (info, place, mask), (low, own, *other), [dense(12)], [scratch(9), scratch(12)], "own"
    )
    low, current = lax.optimization_barrier((low, current))
    current_low, sent = call(
        low_second_kernel, (mask,), (far, low, ready, *parts), [dense(8), packed], [scratch(8), scratch(12)], "low_second"
    )
    current_other = swapped(sent)
    ready, *parts = call(
        last_first_kernel, (mask,), (current_low, current), [dense(4), *partial_sums(LAST)], [], "last_first"
    )
    (out,) = call(
        last_second_kernel, (info, place, mask), (current, current_other, ready, *parts),
        [jax.ShapeDtypeStruct(tiles.shape, tiles.dtype)], [scratch(8), scratch(12), scratch(13)], "last_second",
    )
    return out


def solution(mesh):
    return jax.shard_map(
        per_device,
        mesh=mesh,
        in_specs=(P("grp", None), P(("grp", "dev"), None, None, None)),
        out_specs=P(("grp", "dev"), None, None, None),
        check_vma=False,
    )
```

```python
import functools

import jax
import jax.numpy as jnp
from jax import lax
from jax.experimental import pallas as pl
from jax.experimental.pallas import tpu as pltpu
from jax.sharding import PartitionSpec as P

BS = 128
ROWS = 4
HALF = 4
FAR = 8
WINDOW = 16
TILE = 2 * BS


def start_of(row):
    return 5 * row + row * (row - 1) // 2


PACKED = start_of(ROWS)
SLOTS = 2 * HALF


def block(index, first=0):
    return pl.ds((index - first) * BS, BS)


def lanes(index, first=0):
    return pl.ds(pl.multiple_of((index - first) * BS, BS), BS)


def tile(index, first=0):
    return pl.ds((2 * index - first) * BS, TILE)


def local_row(info_ref, row):
    return jnp.where(info_ref[1] > 0, row, ROWS - 1 - row)


def pack_kernel(info_ref, cols_ref, tiles_ref, out_ref, table_ref, sem):
    total = cols_ref.shape[1]
    table = pltpu.make_async_copy(cols_ref, table_ref, sem)
    table.start()
    out_ref[...] = jnp.zeros_like(out_ref)
    table.wait()
    base, sign = info_ref[0], info_ref[1]
    copies = []
    for row in range(ROWS):
        held = local_row(info_ref, row)
        for slot in range(SLOTS):
            column = table_ref[slot, base + sign * row]
            where = lax.rem(sign * (column - base) + total, total)
            wanted = (column < total) & (where < HALF + ROWS)
            target = jnp.where(wanted, start_of(row) + where, 0)
            copy = pltpu.make_async_copy(tiles_ref.at[held, slot], out_ref.at[target], sem)
            copies.append((wanted, copy))
            pl.when(wanted)(copy.start)
    for wanted, copy in copies:
        pl.when(wanted)(copy.wait)


def spread(info_ref, place_ref, sources, index, target_ref, first_column):
    last = target_ref.shape[1] // BS - 1
    count = ROWS // len(sources)
    for row in range(ROWS):
        held = local_row(info_ref, row)
        for slot in range(SLOTS):
            where = jnp.minimum(place_ref[(index + row) * SLOTS + slot] - first_column, last)
            value = sources[0][held % count, slot]
            for i in range(1, len(sources)):
                value = jnp.where(held >= i * count, sources[i][held % count, slot], value)
            target_ref[block(row), lanes(where)] = value


def kept(value, mask_ref, row_pair, column_pair):
    parts = []
    for down in range(2):
        across = []
        for right in range(2):
            one = value[down * BS:(down + 1) * BS, right * BS:(right + 1) * BS]
            there = mask_ref[(2 * row_pair + down) * WINDOW + 2 * column_pair + right] > 0
            across.append(jnp.where(there, one, jnp.zeros_like(one)))
        parts.append(jnp.concatenate(across, axis=1))
    return jnp.concatenate(parts, axis=0)


class Dense:
    def __init__(self, ref, first_row, first_column):
        self.ref, self.first_row, self.first_column = ref, first_row, first_column

    def rows(self, row_pair, count=1):
        return pl.ds((2 * row_pair - self.first_row) * BS, count * TILE)

    def columns(self, column_pair, count=1):
        return pl.ds((2 * column_pair - self.first_column) * BS, count * TILE)

    def __getitem__(self, at):
        return self.ref[self.rows(at[0]), self.columns(at[1])]

    def __setitem__(self, at, value):
        self.ref[self.rows(at[0]), self.columns(at[1])] = value


def product(left, right, row_pair, column_pair, ks):
    ks = [k for k in sorted(ks) if abs(k - row_pair) <= 2 and abs(k - column_pair) <= 2]
    total = None
    while ks:
        source = right[ks[0]]
        count = 1
        while count < len(ks) and ks[count] == ks[0] + count and right[ks[count]].ref is source.ref:
            count += 1
        part = jnp.dot(
            left.ref[left.rows(row_pair), left.columns(ks[0], count)],
            source.ref[source.rows(ks[0], count), source.columns(column_pair)],
            preferred_element_type=jnp.float32,
        )
        total = part if total is None else total + part
        ks = ks[count:]
    return total


class Step:
    def __init__(self, pairs, low, high, early, late, wanted):
        self.pairs, self.low, self.high, self.early, self.late, self.wanted = pairs, low, high, early, late, wanted

    def columns(self, row_pair):
        return range(max(row_pair - 2, self.low), min(row_pair + 2, self.high) + 1)

    def whole(self, row_pair, column_pair):
        return not any(abs(k - row_pair) <= 2 and abs(k - column_pair) <= 2 for k in self.late)

    def open(self):
        squares = [(p, c) for p in self.pairs for c in self.columns(p) if not self.whole(p, c)]
        cubes = [(p, c) for p in self.pairs for c in self.wanted(p) if self.done(p, c)]
        return {at: i for i, at in enumerate(squares)}, {at: i for i, at in enumerate(cubes)}

    def done(self, row_pair, column_pair):
        return [k for k in self.columns(row_pair) if self.whole(row_pair, k) and abs(k - column_pair) <= 2]

    def first(self, left, right, square, mask_ref, square_part, cube_part):
        squares, cubes = self.open()
        for p in self.pairs:
            for c in self.columns(p):
                value = product(left, right, p, c, self.early)
                if (p, c) in squares:
                    square_part[squares[p, c]] = value
                else:
                    square[p, c] = kept(value, mask_ref, p, c).astype(jnp.bfloat16)
        for (p, c), i in cubes.items():
            cube_part[i] = product(square, right, p, c, self.done(p, c))

    def second(self, left, right, square, ready, mask_ref, square_part, cube_part, write, finish=lambda p: None):
        squares, cubes = self.open()
        for (p, c), i in squares.items():
            value = square_part[i] + product(left, right, p, c, self.late)
            square[p, c] = kept(value, mask_ref, p, c).astype(jnp.bfloat16)
        for p in self.pairs:
            for c in self.wanted(p):
                rest = [k for k in self.columns(p) if not self.whole(p, k)]
                cube = product(square, right, p, c, rest)
                if (p, c) in cubes:
                    cube = cube_part[cubes[p, c]] if cube is None else cube_part[cubes[p, c]] + cube
                own = (square if (p, c) in squares else ready)[p, c].astype(jnp.float32)
                write(p, c, (3.0 * own - 2.0 * kept(cube, mask_ref, p, c)).astype(jnp.bfloat16))
            finish(p)

    def all(self, left, right, square, mask_ref, write):
        for p in self.pairs:
            for c in self.columns(p):
                value = product(left, right, p, c, self.early)
                square[p, c] = kept(value, mask_ref, p, c).astype(jnp.bfloat16)
        for p in self.pairs:
            for c in self.wanted(p):
                cube = product(square, right, p, c, self.early)
                own = square[p, c].astype(jnp.float32)
                write(p, c, (3.0 * own - 2.0 * kept(cube, mask_ref, p, c)).astype(jnp.bfloat16))


OWN = Step((4, 5), 2, 7, (2, 3, 4, 5, 6, 7), (), lambda p: range(p - 2, p + 3))
LOW = Step((2, 3), 0, 5, (2, 3, 4, 5), (0, 1), lambda p: range(2, p + 3))
LAST = Step((4, 5), 2, 7, (2, 3, 4, 5), (6, 7), lambda p: range(p - 2, p + 3))


def own_rows_kernel(info_ref, place_ref, tiles_ref, own_ref):
    own_ref[...] = jnp.zeros_like(own_ref)
    spread(info_ref, place_ref, (tiles_ref,), 8, own_ref, 4)


def low_first_kernel(info_ref, place_ref, mask_ref, near_ref, own_ref, low_ref, square_ref, square_part, cube_part):
    low_ref[...] = jnp.zeros_like(low_ref)
    spread(info_ref, place_ref, (near_ref,), 4, low_ref, 0)
    low, own = Dense(low_ref, 4, 0), Dense(own_ref, 8, 4)
    LOW.first(low, {2: low, 3: low, 4: own, 5: own}, Dense(square_ref, 4, 8), mask_ref, square_part, cube_part)


def own_kernel(info_ref, place_ref, mask_ref, low_ref, own_ref, other0_ref, other1_ref, next_ref, high_ref, square_ref):
    high_ref[...] = jnp.zeros_like(high_ref)
    spread(info_ref, place_ref, (other0_ref, other1_ref), 12, high_ref, 8)
    low, own, high = Dense(low_ref, 4, 0), Dense(own_ref, 8, 4), Dense(high_ref, 12, 8)
    result = Dense(next_ref, 8, 4)
    next_ref[tile(4, 8), tile(7, 4)] = jnp.zeros((TILE, TILE), jnp.bfloat16)
    next_ref[tile(5, 8), tile(2, 4)] = jnp.zeros((TILE, TILE), jnp.bfloat16)

    def write(p, c, value):
        result[p, c] = value

    OWN.all(own, {2: low, 3: low, 4: own, 5: own, 6: high, 7: high}, Dense(square_ref, 8, 4), mask_ref, write)


def low_second_kernel(mask_ref, far_ref, low_ref, ready_ref, square_part, cube_part, sent_ref, far_dense_ref, square_ref):
    for row in range(ROWS):
        for column in range(8):
            if column < row + 5:
                far_dense_ref[block(row), block(column)] = far_ref[start_of(row) + column]
            else:
                far_dense_ref[block(row), block(column)] = jnp.zeros((BS, BS), jnp.bfloat16)
    low, far = Dense(low_ref, 4, 0), Dense(far_dense_ref, 0, 0)

    def write(p, c, value):
        for down in range(2):
            for right in range(2):
                row, column = 2 * p + down - 4, 2 * c + right - 4
                if column < row + 5:
                    sent_ref[start_of(row) + column] = value[down * BS:(down + 1) * BS, right * BS:(right + 1) * BS]

    LOW.second(
        low, {0: far, 1: far, 2: low, 3: low}, Dense(square_ref, 4, 0), Dense(ready_ref, 4, 8), mask_ref,
        square_part, cube_part, write,
    )


def last_first_kernel(mask_ref, sent_ref, own_ref, square_ref, square_part, cube_part, low_ref):
    for row in range(ROWS):
        for column in range(8):
            if column < row + 5:
                low_ref[block(row), block(column)] = sent_ref[start_of(row) + column]
            else:
                low_ref[block(row), block(column)] = jnp.zeros((BS, BS), jnp.bfloat16)
    low, own = Dense(low_ref, 4, 4), Dense(own_ref, 8, 4)
    LAST.first(own, {2: low, 3: low, 4: own, 5: own}, Dense(square_ref, 8, 4), mask_ref, square_part, cube_part)


def last_second_kernel(info_ref, place_ref, mask_ref, own_ref, other_ref, ready_ref, square_part, cube_part,
                       out_ref, high_ref, square_ref, dense_ref, rows_ref, sems):
    for row in range(ROWS):
        for column in range(8):
            if column < row + 5:
                high_ref[block(3 - row), block(7 - column)] = other_ref[start_of(row) + column]
            else:
                high_ref[block(3 - row), block(7 - column)] = jnp.zeros((BS, BS), jnp.bfloat16)
    own, high = Dense(own_ref, 8, 4), Dense(high_ref, 12, 8)
    result = Dense(dense_ref, 8, 4)
    empty = dense_ref.shape[1] // BS - 1
    dense_ref[:, block(empty)] = jnp.zeros((ROWS * BS, BS), jnp.bfloat16)

    def write(p, c, value):
        result[p, c] = value

    copies = []

    def finish(p):
        for row in (2 * p - 8, 2 * p - 7):
            for slot in range(SLOTS):
                where = place_ref[(8 + row) * SLOTS + slot] - 4
                rows_ref[row, slot] = dense_ref[block(row), lanes(jnp.minimum(where, empty))]
            copies.append(pltpu.make_async_copy(rows_ref.at[row], out_ref.at[local_row(info_ref, row)], sems.at[row]))
            copies[-1].start()

    LAST.second(
        own, {4: own, 5: own, 6: high, 7: high}, Dense(square_ref, 8, 4), Dense(ready_ref, 8, 4), mask_ref,
        square_part, cube_part, write, finish,
    )
    for copy in copies:
        copy.wait()


def call(kernel, scalars, operands, outs, scratch, name, space=pltpu.VMEM, limit=12, out_space=pltpu.VMEM):
    smem, vmem = pl.BlockSpec(memory_space=pltpu.SMEM), pl.BlockSpec(memory_space=pltpu.VMEM)
    return pl.pallas_call(
        kernel,
        out_shape=outs,
        in_specs=[smem] * len(scalars) + [pl.BlockSpec(memory_space=space)] * len(operands),
        out_specs=[pl.BlockSpec(memory_space=out_space)] * len(outs),
        scratch_shapes=scratch,
        compiler_params=pltpu.CompilerParams(vmem_limit_bytes=limit * 2**20),
        cost_estimate=pl.CostEstimate(flops=0, bytes_accessed=0, transcendentals=0),
        name=name,
    )(*scalars, *operands)


def dense(columns, rows=ROWS):
    return jax.ShapeDtypeStruct((rows * BS, columns * BS), jnp.bfloat16)


def partial_sums(step):
    return [jax.ShapeDtypeStruct((len(part), TILE, TILE), jnp.float32) for part in step.open()]


def scratch(columns, rows=ROWS):
    return pltpu.VMEM((rows * BS, columns * BS), jnp.bfloat16)


def per_device(cols, tiles):
    devices = lax.axis_size("dev")
    total = cols.shape[0]
    layer = lax.axis_index("layer")
    base = lax.axis_index("dev") * ROWS + layer * (ROWS - 1)
    sign = 1 - 2 * layer
    info = jnp.stack([base, sign]).astype(jnp.int32)
    axes = ("dev", "layer")

    def shifted(value, step):
        pairs = []
        for i in range(devices):
            pairs.append((2 * i, (i + step) % devices * 2))
            pairs.append((2 * i + 1, (i - step) % devices * 2 + 1))
        return lax.ppermute(value, axes, pairs)

    def swapped(value):
        return lax.ppermute(value, "layer", [(0, 1), (1, 0)])

    near = shifted(tiles, 1)
    packed = jax.ShapeDtypeStruct((PACKED, BS, BS), jnp.bfloat16)
    (packed_rows,) = call(
        pack_kernel, (info,), (cols.T, tiles), [packed],
        [pltpu.SMEM(cols.T.shape, jnp.int32), pltpu.SemaphoreType.DMA], "pack", pltpu.HBM, 56,
    )
    far = shifted(packed_rows, 2)
    rows = (base + sign * (jnp.arange(WINDOW, dtype=jnp.int32) - FAR) + total) % total
    window = jnp.take(cols, rows, axis=0)
    where = (sign * (window - base) + FAR + 2 * total) % total
    where = jnp.where((window < total) & (where < WINDOW), where, WINDOW)
    place = where.reshape(-1)
    pattern = jnp.any(where[:, :, None] == jnp.arange(WINDOW, dtype=jnp.int32), axis=1)
    mask = pattern.astype(jnp.int32).reshape(-1)

    (own,) = call(own_rows_kernel, (info, place), (tiles,), [dense(13)], [], "own_rows")

    near, packed_rows, own, mask = lax.optimization_barrier((near, packed_rows, own, mask))
    other = [swapped(near[:2]), swapped(near[2:])]
    low, ready, *parts = call(
        low_first_kernel, (info, place, mask), (near, own), [dense(13), dense(4), *partial_sums(LOW)], [], "low_first"
    )
    (current,) = call(
        own_kernel, (info, place, mask), (low, own, *other), [dense(12)], [scratch(9), scratch(12)], "own"
    )
    low, current = lax.optimization_barrier((low, current))
    (sent,) = call(
        low_second_kernel, (mask,), (far, low, ready, *parts), [packed], [scratch(8), scratch(12)], "low_second"
    )
    current_other = swapped(sent)
    ready, *parts = call(
        last_first_kernel, (mask,), (sent, current), [dense(4), *partial_sums(LAST)], [scratch(8)], "last_first"
    )
    (out,) = call(
        last_second_kernel, (info, place, mask), (current, current_other, ready, *parts),
        [jax.ShapeDtypeStruct(tiles.shape, tiles.dtype)], [scratch(8), scratch(12), scratch(13),
         pltpu.VMEM(tiles.shape, tiles.dtype), pltpu.SemaphoreType.DMA((ROWS,))],
        "last_second", out_space=pltpu.HBM,
    )
    return out


def solution(mesh):
    return jax.shard_map(
        per_device,
        mesh=mesh,
        in_specs=(P("grp", None), P(("grp", "dev"), None, None, None)),
        out_specs=P(("grp", "dev"), None, None, None),
        check_vma=False,
    )
```

```python
import functools

import jax
import jax.numpy as jnp
from jax import lax
from jax.experimental import pallas as pl
from jax.experimental.pallas import tpu as pltpu
from jax.sharding import PartitionSpec as P

BS = 128
ROWS = 4
HALF = 4
FAR = 8
WINDOW = 16
TILE = 2 * BS


def start_of(row):
    return 5 * row + row * (row - 1) // 2


PACKED = start_of(ROWS)
SLOTS = 2 * HALF


def block(index, first=0):
    return pl.ds((index - first) * BS, BS)


def lanes(index, first=0):
    return pl.ds(pl.multiple_of((index - first) * BS, BS), BS)


def tile(index, first=0):
    return pl.ds((2 * index - first) * BS, TILE)


def local_row(info_ref, row):
    return jnp.where(info_ref[1] > 0, row, ROWS - 1 - row)


def pack_kernel(info_ref, cols_ref, tiles_ref, out_ref, table_ref, sem):
    total = cols_ref.shape[1]
    table = pltpu.make_async_copy(cols_ref, table_ref, sem)
    table.start()
    out_ref[...] = jnp.zeros_like(out_ref)
    table.wait()
    base, sign = info_ref[0], info_ref[1]
    copies = []
    for row in range(ROWS):
        held = local_row(info_ref, row)
        for slot in range(SLOTS):
            column = table_ref[slot, base + sign * row]
            where = lax.rem(sign * (column - base) + total, total)
            wanted = (column < total) & (where < HALF + ROWS)
            target = jnp.where(wanted, start_of(row) + where, 0)
            copy = pltpu.make_async_copy(tiles_ref.at[held, slot], out_ref.at[target], sem)
            copies.append((wanted, copy))
            pl.when(wanted)(copy.start)
    for wanted, copy in copies:
        pl.when(wanted)(copy.wait)


def spread(info_ref, place_ref, sources, index, target_ref, first_column):
    last = target_ref.shape[1] // BS - 1
    count = ROWS // len(sources)
    for row in range(ROWS):
        held = local_row(info_ref, row)
        for slot in range(SLOTS):
            where = jnp.minimum(place_ref[(index + row) * SLOTS + slot] - first_column, last)
            value = sources[0][held % count, slot]
            for i in range(1, len(sources)):
                value = jnp.where(held >= i * count, sources[i][held % count, slot], value)
            target_ref[block(row), lanes(where)] = value


def kept(value, mask_ref, row_pair, column_pair):
    parts = []
    for down in range(2):
        across = []
        for right in range(2):
            one = value[down * BS:(down + 1) * BS, right * BS:(right + 1) * BS]
            there = mask_ref[(2 * row_pair + down) * WINDOW + 2 * column_pair + right] > 0
            across.append(jnp.where(there, one, jnp.zeros_like(one)))
        parts.append(jnp.concatenate(across, axis=1))
    return jnp.concatenate(parts, axis=0)


class Dense:
    def __init__(self, ref, first_row, first_column):
        self.ref, self.first_row, self.first_column = ref, first_row, first_column

    def rows(self, row_pair, count=1):
        return pl.ds((2 * row_pair - self.first_row) * BS, count * TILE)

    def columns(self, column_pair, count=1):
        return pl.ds((2 * column_pair - self.first_column) * BS, count * TILE)

    def __getitem__(self, at):
        return self.ref[self.rows(at[0]), self.columns(at[1])]

    def __setitem__(self, at, value):
        self.ref[self.rows(at[0]), self.columns(at[1])] = value


def product(left, right, row_pair, column_pair, ks):
    ks = [k for k in sorted(ks) if abs(k - row_pair) <= 2 and abs(k - column_pair) <= 2]
    total = None
    while ks:
        source = right[ks[0]]
        count = 1
        while count < len(ks) and ks[count] == ks[0] + count and right[ks[count]].ref is source.ref:
            count += 1
        part = jnp.dot(
            left.ref[left.rows(row_pair), left.columns(ks[0], count)],
            source.ref[source.rows(ks[0], count), source.columns(column_pair)],
            preferred_element_type=jnp.float32,
        )
        total = part if total is None else total + part
        ks = ks[count:]
    return total


class Step:
    def __init__(self, pairs, low, high, early, late, wanted):
        self.pairs, self.low, self.high, self.early, self.late, self.wanted = pairs, low, high, early, late, wanted

    def columns(self, row_pair):
        return range(max(row_pair - 2, self.low), min(row_pair + 2, self.high) + 1)

    def whole(self, row_pair, column_pair):
        return not any(abs(k - row_pair) <= 2 and abs(k - column_pair) <= 2 for k in self.late)

    def open(self):
        squares = [(p, c) for p in self.pairs for c in self.columns(p) if not self.whole(p, c)]
        cubes = [(p, c) for p in self.pairs for c in self.wanted(p) if self.done(p, c)]
        return {at: i for i, at in enumerate(squares)}, {at: i for i, at in enumerate(cubes)}

    def done(self, row_pair, column_pair):
        return [k for k in self.columns(row_pair) if self.whole(row_pair, k) and abs(k - column_pair) <= 2]

    def first(self, left, right, square, mask_ref, square_part, cube_part):
        squares, cubes = self.open()
        for p in self.pairs:
            for c in self.columns(p):
                value = product(left, right, p, c, self.early)
                if (p, c) in squares:
                    square_part[squares[p, c]] = value
                else:
                    square[p, c] = kept(value, mask_ref, p, c).astype(jnp.bfloat16)
        for (p, c), i in cubes.items():
            cube_part[i] = product(square, right, p, c, self.done(p, c))

    def second(self, left, right, square, ready, mask_ref, square_part, cube_part, write, finish=lambda p: None):
        squares, cubes = self.open()
        for (p, c), i in squares.items():
            value = square_part[i] + product(left, right, p, c, self.late)
            square[p, c] = kept(value, mask_ref, p, c).astype(jnp.bfloat16)
        for p in self.pairs:
            for c in self.wanted(p):
                rest = [k for k in self.columns(p) if not self.whole(p, k)]
                cube = product(square, right, p, c, rest)
                if (p, c) in cubes:
                    cube = cube_part[cubes[p, c]] if cube is None else cube_part[cubes[p, c]] + cube
                own = (square if (p, c) in squares else ready)[p, c].astype(jnp.float32)
                write(p, c, (3.0 * own - 2.0 * kept(cube, mask_ref, p, c)).astype(jnp.bfloat16))
            finish(p)

    def all(self, left, right, square, mask_ref, write):
        for p in self.pairs:
            for c in self.columns(p):
                value = product(left, right, p, c, self.early)
                square[p, c] = kept(value, mask_ref, p, c).astype(jnp.bfloat16)
        for p in self.pairs:
            for c in self.wanted(p):
                cube = product(square, right, p, c, self.early)
                own = square[p, c].astype(jnp.float32)
                write(p, c, (3.0 * own - 2.0 * kept(cube, mask_ref, p, c)).astype(jnp.bfloat16))


OWN = Step((4, 5), 2, 7, (2, 3, 4, 5, 6, 7), (), lambda p: range(p - 2, p + 3))
LOW = Step((2, 3), 0, 5, (2, 3, 4, 5), (0, 1), lambda p: range(2, p + 3))
LAST = Step((4, 5), 2, 7, (2, 3, 4, 5), (6, 7), lambda p: range(p - 2, p + 3))


def own_rows_kernel(info_ref, place_ref, tiles_ref, own_ref):
    own_ref[...] = jnp.zeros_like(own_ref)
    spread(info_ref, place_ref, (tiles_ref,), 8, own_ref, 4)


def low_first_kernel(info_ref, place_ref, mask_ref, near_ref, own_ref, low_ref, square_ref, square_part, cube_part):
    low_ref[...] = jnp.zeros_like(low_ref)
    spread(info_ref, place_ref, (near_ref,), 4, low_ref, 0)
    low, own = Dense(low_ref, 4, 0), Dense(own_ref, 8, 4)
    LOW.first(low, {2: low, 3: low, 4: own, 5: own}, Dense(square_ref, 4, 8), mask_ref, square_part, cube_part)


def own_kernel(info_ref, place_ref, mask_ref, low_ref, own_ref, other0_ref, other1_ref, next_ref, high_ref, square_ref):
    high_ref[...] = jnp.zeros_like(high_ref)
    spread(info_ref, place_ref, (other0_ref, other1_ref), 12, high_ref, 8)
    low, own, high = Dense(low_ref, 4, 0), Dense(own_ref, 8, 4), Dense(high_ref, 12, 8)
    result = Dense(next_ref, 8, 4)
    next_ref[tile(4, 8), tile(7, 4)] = jnp.zeros((TILE, TILE), jnp.bfloat16)
    next_ref[tile(5, 8), tile(2, 4)] = jnp.zeros((TILE, TILE), jnp.bfloat16)

    def write(p, c, value):
        result[p, c] = value

    OWN.all(own, {2: low, 3: low, 4: own, 5: own, 6: high, 7: high}, Dense(square_ref, 8, 4), mask_ref, write)


def low_second_kernel(mask_ref, far_ref, low_ref, ready_ref, square_part, cube_part, sent_ref, far_dense_ref, square_ref):
    for row in range(ROWS):
        for column in range(8):
            if column < row + 5:
                far_dense_ref[block(row), block(column)] = far_ref[start_of(row) + column]
            else:
                far_dense_ref[block(row), block(column)] = jnp.zeros((BS, BS), jnp.bfloat16)
    low, far = Dense(low_ref, 4, 0), Dense(far_dense_ref, 0, 0)

    def write(p, c, value):
        for down in range(2):
            for right in range(2):
                row, column = 2 * p + down - 4, 2 * c + right - 4
                if column < row + 5:
                    sent_ref[start_of(row) + column] = value[down * BS:(down + 1) * BS, right * BS:(right + 1) * BS]

    LOW.second(
        low, {0: far, 1: far, 2: low, 3: low}, Dense(square_ref, 4, 0), Dense(ready_ref, 4, 8), mask_ref,
        square_part, cube_part, write,
    )


def last_first_kernel(mask_ref, sent_ref, own_ref, square_ref, square_part, cube_part, low_ref):
    for row in range(ROWS):
        for column in range(8):
            if column < row + 5:
                low_ref[block(row), block(column)] = sent_ref[start_of(row) + column]
            else:
                low_ref[block(row), block(column)] = jnp.zeros((BS, BS), jnp.bfloat16)
    low, own = Dense(low_ref, 4, 4), Dense(own_ref, 8, 4)
    LAST.first(own, {2: low, 3: low, 4: own, 5: own}, Dense(square_ref, 8, 4), mask_ref, square_part, cube_part)


def last_second_kernel(info_ref, place_ref, slot_ref, mask_ref, own_ref, other_ref, ready_ref, square_part, cube_part,
                       out_ref, high_ref, square_ref, dense_ref, empty_ref, sem):
    for row in range(ROWS):
        for column in range(8):
            if column < row + 5:
                high_ref[block(3 - row), block(7 - column)] = other_ref[start_of(row) + column]
            else:
                high_ref[block(3 - row), block(7 - column)] = jnp.zeros((BS, BS), jnp.bfloat16)
    own, high = Dense(own_ref, 8, 4), Dense(high_ref, 12, 8)
    result = Dense(dense_ref, 8, 4)
    empty_ref[...] = jnp.zeros_like(empty_ref)
    for row in range(ROWS):
        for slot in range(SLOTS):
            copy = pltpu.make_async_copy(empty_ref, out_ref.at[local_row(info_ref, row), slot], sem)
            pl.when(place_ref[(8 + row) * SLOTS + slot] >= WINDOW)(copy.start)

    def write(p, c, value):
        result[p, c] = value
        for down in range(2):
            for right in range(2):
                row, column = 2 * p + down, 2 * c + right
                if abs(row - column) > HALF:
                    continue
                slot = slot_ref[(row - 8) * WINDOW + column]
                copy = pltpu.make_async_copy(
                    dense_ref.at[block(row, 8), block(column, 4)],
                    out_ref.at[local_row(info_ref, row - 8), jnp.minimum(slot, SLOTS - 1)], sem,
                )
                pl.when(slot < SLOTS)(copy.start)

    LAST.second(
        own, {4: own, 5: own, 6: high, 7: high}, Dense(square_ref, 8, 4), Dense(ready_ref, 8, 4), mask_ref,
        square_part, cube_part, write,
    )
    pltpu.make_async_copy(out_ref, out_ref, sem).wait()


def call(kernel, scalars, operands, outs, scratch, name, space=pltpu.VMEM, limit=12, out_space=pltpu.VMEM):
    smem, vmem = pl.BlockSpec(memory_space=pltpu.SMEM), pl.BlockSpec(memory_space=pltpu.VMEM)
    return pl.pallas_call(
        kernel,
        out_shape=outs,
        in_specs=[smem] * len(scalars) + [pl.BlockSpec(memory_space=space)] * len(operands),
        out_specs=[pl.BlockSpec(memory_space=out_space)] * len(outs),
        scratch_shapes=scratch,
        compiler_params=pltpu.CompilerParams(vmem_limit_bytes=limit * 2**20),
        cost_estimate=pl.CostEstimate(flops=0, bytes_accessed=0, transcendentals=0),
        name=name,
    )(*scalars, *operands)


def dense(columns, rows=ROWS):
    return jax.ShapeDtypeStruct((rows * BS, columns * BS), jnp.bfloat16)


def partial_sums(step):
    return [jax.ShapeDtypeStruct((len(part), TILE, TILE), jnp.float32) for part in step.open()]


def scratch(columns, rows=ROWS):
    return pltpu.VMEM((rows * BS, columns * BS), jnp.bfloat16)


def per_device(cols, tiles):
    devices = lax.axis_size("dev")
    total = cols.shape[0]
    layer = lax.axis_index("layer")
    base = lax.axis_index("dev") * ROWS + layer * (ROWS - 1)
    sign = 1 - 2 * layer
    info = jnp.stack([base, sign]).astype(jnp.int32)
    axes = ("dev", "layer")

    def shifted(value, step):
        pairs = []
        for i in range(devices):
            pairs.append((2 * i, (i + step) % devices * 2))
            pairs.append((2 * i + 1, (i - step) % devices * 2 + 1))
        return lax.ppermute(value, axes, pairs)

    def swapped(value):
        return lax.ppermute(value, "layer", [(0, 1), (1, 0)])

    near = shifted(tiles, 1)
    packed = jax.ShapeDtypeStruct((PACKED, BS, BS), jnp.bfloat16)
    (packed_rows,) = call(
        pack_kernel, (info,), (cols.T, tiles), [packed],
        [pltpu.SMEM(cols.T.shape, jnp.int32), pltpu.SemaphoreType.DMA], "pack", pltpu.HBM, 56,
    )
    far = shifted(packed_rows, 2)
    rows = (base + sign * (jnp.arange(WINDOW, dtype=jnp.int32) - FAR) + total) % total
    window = jnp.take(cols, rows, axis=0)
    where = (sign * (window - base) + FAR + 2 * total) % total
    where = jnp.where((window < total) & (where < WINDOW), where, WINDOW)
    place = where.reshape(-1)
    match = where[FAR:FAR + ROWS, :, None] == jnp.arange(WINDOW, dtype=jnp.int32)
    slot = jnp.min(jnp.where(match, jnp.arange(SLOTS, dtype=jnp.int32)[None, :, None], SLOTS), axis=1).reshape(-1)
    pattern = jnp.any(where[:, :, None] == jnp.arange(WINDOW, dtype=jnp.int32), axis=1)
    mask = pattern.astype(jnp.int32).reshape(-1)

    (own,) = call(own_rows_kernel, (info, place), (tiles,), [dense(13)], [], "own_rows")

    near, packed_rows, own, mask = lax.optimization_barrier((near, packed_rows, own, mask))
    other = [swapped(near[:2]), swapped(near[2:])]
    low, ready, *parts = call(
        low_first_kernel, (info, place, mask), (near, own), [dense(13), dense(4), *partial_sums(LOW)], [], "low_first"
    )
    (current,) = call(
        own_kernel, (info, place, mask), (low, own, *other), [dense(12)], [scratch(9), scratch(12)], "own"
    )
    low, current = lax.optimization_barrier((low, current))
    (sent,) = call(
        low_second_kernel, (mask,), (far, low, ready, *parts), [packed], [scratch(8), scratch(12)], "low_second"
    )
    current_other = swapped(sent)
    ready, *parts = call(
        last_first_kernel, (mask,), (sent, current), [dense(4), *partial_sums(LAST)], [scratch(8)], "last_first"
    )
    (out,) = call(
        last_second_kernel, (info, place, slot, mask), (current, current_other, ready, *parts),
        [jax.ShapeDtypeStruct(tiles.shape, tiles.dtype)], [scratch(8), scratch(12), scratch(12), pltpu.VMEM((BS, BS), jnp.bfloat16), pltpu.SemaphoreType.DMA],
        "last_second", out_space=pltpu.HBM,
    )
    return out


def solution(mesh):
    return jax.shard_map(
        per_device,
        mesh=mesh,
        in_specs=(P("grp", None), P(("grp", "dev"), None, None, None)),
        out_specs=P(("grp", "dev"), None, None, None),
        check_vma=False,
    )
```

```python
import functools

import jax
import jax.numpy as jnp
from jax import lax
from jax.experimental import pallas as pl
from jax.experimental.pallas import tpu as pltpu
from jax.sharding import PartitionSpec as P

BS = 128
ROWS = 4
HALF = 4
FAR = 8
WINDOW = 16
TILE = 2 * BS


def start_of(row):
    return 5 * row + row * (row - 1) // 2


PACKED = start_of(ROWS)
SLOTS = 2 * HALF


def block(index, first=0):
    return pl.ds((index - first) * BS, BS)


def lanes(index, first=0):
    return pl.ds(pl.multiple_of((index - first) * BS, BS), BS)


def tile(index, first=0):
    return pl.ds((2 * index - first) * BS, TILE)


def local_row(info_ref, row):
    return jnp.where(info_ref[1] > 0, row, ROWS - 1 - row)


def pack_kernel(info_ref, cols_ref, tiles_ref, out_ref, table_ref, sem):
    total = cols_ref.shape[1]
    table = pltpu.make_async_copy(cols_ref, table_ref, sem)
    table.start()
    out_ref[...] = jnp.zeros_like(out_ref)
    table.wait()
    base, sign = info_ref[0], info_ref[1]
    copies = []
    for row in range(ROWS):
        held = local_row(info_ref, row)
        for slot in range(SLOTS):
            column = table_ref[slot, base + sign * row]
            where = lax.rem(sign * (column - base) + total, total)
            wanted = (column < total) & (where < HALF + ROWS)
            target = jnp.where(wanted, start_of(row) + where, 0)
            copy = pltpu.make_async_copy(tiles_ref.at[held, slot], out_ref.at[target], sem)
            copies.append((wanted, copy))
            pl.when(wanted)(copy.start)
    for wanted, copy in copies:
        pl.when(wanted)(copy.wait)


def spread(info_ref, place_ref, sources, index, target_ref, first_column):
    last = target_ref.shape[1] // BS - 1
    count = ROWS // len(sources)
    for row in range(ROWS):
        held = local_row(info_ref, row)
        for slot in range(SLOTS):
            where = jnp.minimum(place_ref[(index + row) * SLOTS + slot] - first_column, last)
            value = sources[0][held % count, slot]
            for i in range(1, len(sources)):
                value = jnp.where(held >= i * count, sources[i][held % count, slot], value)
            target_ref[block(row), lanes(where)] = value


class Part:
    def __init__(self, ref, first):
        self.ref, self.first = ref, first

    def __getitem__(self, at):
        return self.ref[self.first + at]


def tables(ref):
    firsts = (0, 2, 2 + WINDOW * SLOTS, 2 + WINDOW * SLOTS + ROWS * WINDOW)
    return [Part(ref, first) for first in firsts]


def kept(value, mask_ref, row_pair, column_pair):
    parts = []
    for down in range(2):
        across = []
        for right in range(2):
            one = value[down * BS:(down + 1) * BS, right * BS:(right + 1) * BS]
            there = mask_ref[(2 * row_pair + down) * WINDOW + 2 * column_pair + right] > 0
            across.append(jnp.where(there, one, jnp.zeros_like(one)))
        parts.append(jnp.concatenate(across, axis=1))
    return jnp.concatenate(parts, axis=0)


class Dense:
    def __init__(self, ref, first_row, first_column):
        self.ref, self.first_row, self.first_column = ref, first_row, first_column

    def rows(self, row_pair, count=1):
        return pl.ds((2 * row_pair - self.first_row) * BS, count * TILE)

    def columns(self, column_pair, count=1):
        return pl.ds((2 * column_pair - self.first_column) * BS, count * TILE)

    def __getitem__(self, at):
        return self.ref[self.rows(at[0]), self.columns(at[1])]

    def __setitem__(self, at, value):
        self.ref[self.rows(at[0]), self.columns(at[1])] = value


def product(left, right, row_pair, column_pair, ks):
    ks = [k for k in sorted(ks) if abs(k - row_pair) <= 2 and abs(k - column_pair) <= 2]
    total = None
    while ks:
        source = right[ks[0]]
        count = 1
        while count < len(ks) and ks[count] == ks[0] + count and right[ks[count]].ref is source.ref:
            count += 1
        part = jnp.dot(
            left.ref[left.rows(row_pair), left.columns(ks[0], count)],
            source.ref[source.rows(ks[0], count), source.columns(column_pair)],
            preferred_element_type=jnp.float32,
        )
        total = part if total is None else total + part
        ks = ks[count:]
    return total


class Step:
    def __init__(self, pairs, low, high, early, late, wanted):
        self.pairs, self.low, self.high, self.early, self.late, self.wanted = pairs, low, high, early, late, wanted

    def columns(self, row_pair):
        return range(max(row_pair - 2, self.low), min(row_pair + 2, self.high) + 1)

    def whole(self, row_pair, column_pair):
        return not any(abs(k - row_pair) <= 2 and abs(k - column_pair) <= 2 for k in self.late)

    def open(self):
        squares = [(p, c) for p in self.pairs for c in self.columns(p) if not self.whole(p, c)]
        cubes = [(p, c) for p in self.pairs for c in self.wanted(p) if self.done(p, c)]
        return {at: i for i, at in enumerate(squares)}, {at: i for i, at in enumerate(cubes)}

    def done(self, row_pair, column_pair):
        return [k for k in self.columns(row_pair) if self.whole(row_pair, k) and abs(k - column_pair) <= 2]

    def first(self, left, right, square, mask_ref, square_part, cube_part):
        squares, cubes = self.open()
        for p in self.pairs:
            for c in self.columns(p):
                value = product(left, right, p, c, self.early)
                if (p, c) in squares:
                    square_part[squares[p, c]] = value
                else:
                    square[p, c] = kept(value, mask_ref, p, c).astype(jnp.bfloat16)
        for (p, c), i in cubes.items():
            cube_part[i] = product(square, right, p, c, self.done(p, c))

    def second(self, left, right, square, ready, mask_ref, square_part, cube_part, write, finish=lambda p: None):
        squares, cubes = self.open()
        for (p, c), i in squares.items():
            value = square_part[i] + product(left, right, p, c, self.late)
            square[p, c] = kept(value, mask_ref, p, c).astype(jnp.bfloat16)
        for p in self.pairs:
            for c in self.wanted(p):
                rest = [k for k in self.columns(p) if not self.whole(p, k)]
                cube = product(square, right, p, c, rest)
                if (p, c) in cubes:
                    cube = cube_part[cubes[p, c]] if cube is None else cube_part[cubes[p, c]] + cube
                own = (square if (p, c) in squares else ready)[p, c].astype(jnp.float32)
                write(p, c, (3.0 * own - 2.0 * kept(cube, mask_ref, p, c)).astype(jnp.bfloat16))
            finish(p)

    def all(self, left, right, square, mask_ref, write):
        for p in self.pairs:
            for c in self.columns(p):
                value = product(left, right, p, c, self.early)
                square[p, c] = kept(value, mask_ref, p, c).astype(jnp.bfloat16)
        for p in self.pairs:
            for c in self.wanted(p):
                cube = product(square, right, p, c, self.early)
                own = square[p, c].astype(jnp.float32)
                write(p, c, (3.0 * own - 2.0 * kept(cube, mask_ref, p, c)).astype(jnp.bfloat16))


OWN = Step((4, 5), 2, 7, (2, 3, 4, 5, 6, 7), (), lambda p: range(p - 2, p + 3))
LOW = Step((2, 3), 0, 5, (2, 3, 4, 5), (0, 1), lambda p: range(2, p + 3))
LAST = Step((4, 5), 2, 7, (2, 3, 4, 5), (6, 7), lambda p: range(p - 2, p + 3))


def own_rows_kernel(table_ref, tiles_ref, own_ref):
    info_ref, place_ref, _, _ = tables(table_ref)
    own_ref[...] = jnp.zeros_like(own_ref)
    spread(info_ref, place_ref, (tiles_ref,), 8, own_ref, 4)


def low_first_kernel(table_ref, near_ref, own_ref, low_ref, square_ref, square_part, cube_part):
    info_ref, place_ref, _, mask_ref = tables(table_ref)
    low_ref[...] = jnp.zeros_like(low_ref)
    spread(info_ref, place_ref, (near_ref,), 4, low_ref, 0)
    low, own = Dense(low_ref, 4, 0), Dense(own_ref, 8, 4)
    LOW.first(low, {2: low, 3: low, 4: own, 5: own}, Dense(square_ref, 4, 8), mask_ref, square_part, cube_part)


def own_kernel(table_ref, low_ref, own_ref, other0_ref, other1_ref, next_ref, high_ref, square_ref):
    info_ref, place_ref, _, mask_ref = tables(table_ref)
    high_ref[...] = jnp.zeros_like(high_ref)
    spread(info_ref, place_ref, (other0_ref, other1_ref), 12, high_ref, 8)
    low, own, high = Dense(low_ref, 4, 0), Dense(own_ref, 8, 4), Dense(high_ref, 12, 8)
    result = Dense(next_ref, 8, 4)
    next_ref[tile(4, 8), tile(7, 4)] = jnp.zeros((TILE, TILE), jnp.bfloat16)
    next_ref[tile(5, 8), tile(2, 4)] = jnp.zeros((TILE, TILE), jnp.bfloat16)

    def write(p, c, value):
        result[p, c] = value

    OWN.all(own, {2: low, 3: low, 4: own, 5: own, 6: high, 7: high}, Dense(square_ref, 8, 4), mask_ref, write)


def low_second_kernel(table_ref, far_ref, low_ref, ready_ref, square_part, cube_part, sent_ref, far_dense_ref, square_ref):
    _, _, _, mask_ref = tables(table_ref)
    for row in range(ROWS):
        for column in range(8):
            if column < row + 5:
                far_dense_ref[block(row), block(column)] = far_ref[start_of(row) + column]
            else:
                far_dense_ref[block(row), block(column)] = jnp.zeros((BS, BS), jnp.bfloat16)
    low, far = Dense(low_ref, 4, 0), Dense(far_dense_ref, 0, 0)

    def write(p, c, value):
        for down in range(2):
            for right in range(2):
                row, column = 2 * p + down - 4, 2 * c + right - 4
                if column < row + 5:
                    sent_ref[start_of(row) + column] = value[down * BS:(down + 1) * BS, right * BS:(right + 1) * BS]

    LOW.second(
        low, {0: far, 1: far, 2: low, 3: low}, Dense(square_ref, 4, 0), Dense(ready_ref, 4, 8), mask_ref,
        square_part, cube_part, write,
    )


def last_first_kernel(table_ref, sent_ref, own_ref, square_ref, square_part, cube_part, low_ref):
    _, _, _, mask_ref = tables(table_ref)
    for row in range(ROWS):
        for column in range(8):
            if column < row + 5:
                low_ref[block(row), block(column)] = sent_ref[start_of(row) + column]
            else:
                low_ref[block(row), block(column)] = jnp.zeros((BS, BS), jnp.bfloat16)
    low, own = Dense(low_ref, 4, 4), Dense(own_ref, 8, 4)
    LAST.first(own, {2: low, 3: low, 4: own, 5: own}, Dense(square_ref, 8, 4), mask_ref, square_part, cube_part)


def last_second_kernel(table_ref, own_ref, other_ref, ready_ref, square_part, cube_part,
                       out_ref, high_ref, square_ref, dense_ref, empty_ref, sem):
    info_ref, place_ref, slot_ref, mask_ref = tables(table_ref)
    for row in range(ROWS):
        for column in range(8):
            if column < row + 5:
                high_ref[block(3 - row), block(7 - column)] = other_ref[start_of(row) + column]
            else:
                high_ref[block(3 - row), block(7 - column)] = jnp.zeros((BS, BS), jnp.bfloat16)
    own, high = Dense(own_ref, 8, 4), Dense(high_ref, 12, 8)
    result = Dense(dense_ref, 8, 4)
    empty_ref[...] = jnp.zeros_like(empty_ref)
    for row in range(ROWS):
        for slot in range(SLOTS):
            copy = pltpu.make_async_copy(empty_ref, out_ref.at[local_row(info_ref, row), slot], sem)
            pl.when(place_ref[(8 + row) * SLOTS + slot] >= WINDOW)(copy.start)

    def write(p, c, value):
        result[p, c] = value
        for down in range(2):
            for right in range(2):
                row, column = 2 * p + down, 2 * c + right
                if abs(row - column) > HALF:
                    continue
                slot = slot_ref[(row - 8) * WINDOW + column]
                copy = pltpu.make_async_copy(
                    dense_ref.at[block(row, 8), block(column, 4)],
                    out_ref.at[local_row(info_ref, row - 8), jnp.minimum(slot, SLOTS - 1)], sem,
                )
                pl.when(slot < SLOTS)(copy.start)

    LAST.second(
        own, {4: own, 5: own, 6: high, 7: high}, Dense(square_ref, 8, 4), Dense(ready_ref, 8, 4), mask_ref,
        square_part, cube_part, write,
    )
    pltpu.make_async_copy(out_ref, out_ref, sem).wait()


def call(kernel, scalars, operands, outs, scratch, name, space=pltpu.VMEM, limit=12, out_space=pltpu.VMEM):
    smem, vmem = pl.BlockSpec(memory_space=pltpu.SMEM), pl.BlockSpec(memory_space=pltpu.VMEM)
    return pl.pallas_call(
        kernel,
        out_shape=outs,
        in_specs=[smem] * len(scalars) + [pl.BlockSpec(memory_space=space)] * len(operands),
        out_specs=[pl.BlockSpec(memory_space=out_space)] * len(outs),
        scratch_shapes=scratch,
        compiler_params=pltpu.CompilerParams(vmem_limit_bytes=limit * 2**20),
        cost_estimate=pl.CostEstimate(flops=0, bytes_accessed=0, transcendentals=0),
        name=name,
    )(*scalars, *operands)


def dense(columns, rows=ROWS):
    return jax.ShapeDtypeStruct((rows * BS, columns * BS), jnp.bfloat16)


def partial_sums(step):
    return [jax.ShapeDtypeStruct((len(part), TILE, TILE), jnp.float32) for part in step.open()]


def scratch(columns, rows=ROWS):
    return pltpu.VMEM((rows * BS, columns * BS), jnp.bfloat16)


def per_device(cols, tiles):
    devices = lax.axis_size("dev")
    total = cols.shape[0]
    layer = lax.axis_index("layer")
    base = lax.axis_index("dev") * ROWS + layer * (ROWS - 1)
    sign = 1 - 2 * layer
    info = jnp.stack([base, sign]).astype(jnp.int32)
    axes = ("dev", "layer")

    def shifted(value, step):
        pairs = []
        for i in range(devices):
            pairs.append((2 * i, (i + step) % devices * 2))
            pairs.append((2 * i + 1, (i - step) % devices * 2 + 1))
        return lax.ppermute(value, axes, pairs)

    def swapped(value):
        return lax.ppermute(value, "layer", [(0, 1), (1, 0)])

    near = shifted(tiles, 1)
    packed = jax.ShapeDtypeStruct((PACKED, BS, BS), jnp.bfloat16)
    (packed_rows,) = call(
        pack_kernel, (info,), (cols.T, tiles), [packed],
        [pltpu.SMEM(cols.T.shape, jnp.int32), pltpu.SemaphoreType.DMA], "pack", pltpu.HBM, 56,
    )
    far = shifted(packed_rows, 2)
    rows = (base + sign * (jnp.arange(WINDOW, dtype=jnp.int32) - FAR) + total) % total
    window = jnp.take(cols, rows, axis=0)
    where = (sign * (window - base) + FAR + 2 * total) % total
    where = jnp.where((window < total) & (where < WINDOW), where, WINDOW)
    place = where.reshape(-1)
    match = where[FAR:FAR + ROWS, :, None] == jnp.arange(WINDOW, dtype=jnp.int32)
    slot = jnp.min(jnp.where(match, jnp.arange(SLOTS, dtype=jnp.int32)[None, :, None], SLOTS), axis=1).reshape(-1)
    pattern = jnp.any(where[:, :, None] == jnp.arange(WINDOW, dtype=jnp.int32), axis=1)
    mask = pattern.astype(jnp.int32).reshape(-1)
    table = jnp.concatenate([info, place, slot, mask])

    (own,) = call(own_rows_kernel, (table,), (tiles,), [dense(13)], [], "own_rows")

    near, packed_rows, own = lax.optimization_barrier((near, packed_rows, own))
    other = [swapped(near[:2]), swapped(near[2:])]
    low, ready, *parts = call(
        low_first_kernel, (table,), (near, own), [dense(13), dense(4), *partial_sums(LOW)], [], "low_first"
    )
    (current,) = call(
        own_kernel, (table,), (low, own, *other), [dense(12)], [scratch(9), scratch(12)], "own"
    )
    low, current = lax.optimization_barrier((low, current))
    (sent,) = call(
        low_second_kernel, (table,), (far, low, ready, *parts), [packed], [scratch(8), scratch(12)], "low_second"
    )
    current_other = swapped(sent)
    ready, *parts = call(
        last_first_kernel, (table,), (sent, current), [dense(4), *partial_sums(LAST)], [scratch(8)], "last_first"
    )
    (out,) = call(
        last_second_kernel, (table,), (current, current_other, ready, *parts),
        [jax.ShapeDtypeStruct(tiles.shape, tiles.dtype)], [scratch(8), scratch(12), scratch(12), pltpu.VMEM((BS, BS), jnp.bfloat16), pltpu.SemaphoreType.DMA],
        "last_second", out_space=pltpu.HBM,
    )
    return out


def solution(mesh):
    return jax.shard_map(
        per_device,
        mesh=mesh,
        in_specs=(P("grp", None), P(("grp", "dev"), None, None, None)),
        out_specs=P(("grp", "dev"), None, None, None),
        check_vma=False,
    )
```

```python
import functools

import jax
import jax.numpy as jnp
from jax import lax
from jax.experimental import pallas as pl
from jax.experimental.pallas import tpu as pltpu
from jax.sharding import PartitionSpec as P

BS = 128
ROWS = 4
HALF = 4
FAR = 8
WINDOW = 16
TILE = 2 * BS


def start_of(row):
    return 5 * row + row * (row - 1) // 2


PACKED = start_of(ROWS)
SLOTS = 2 * HALF


def block(index, first=0):
    return pl.ds((index - first) * BS, BS)


def lanes(index, first=0):
    return pl.ds(pl.multiple_of((index - first) * BS, BS), BS)


def tile(index, first=0):
    return pl.ds((2 * index - first) * BS, TILE)


def local_row(info_ref, row):
    return jnp.where(info_ref[1] > 0, row, ROWS - 1 - row)


def pack_kernel(info_ref, cols_ref, tiles_ref, out_ref, table_ref, sem):
    total = cols_ref.shape[1]
    table = pltpu.make_async_copy(cols_ref, table_ref, sem)
    table.start()
    out_ref[...] = jnp.zeros_like(out_ref)
    table.wait()
    base, sign = info_ref[0], info_ref[1]
    copies = []
    for row in range(ROWS):
        held = local_row(info_ref, row)
        for slot in range(SLOTS):
            column = table_ref[slot, base + sign * row]
            where = lax.rem(sign * (column - base) + total, total)
            wanted = (column < total) & (where < HALF + ROWS)
            target = jnp.where(wanted, start_of(row) + where, 0)
            copy = pltpu.make_async_copy(tiles_ref.at[held, slot], out_ref.at[target], sem)
            copies.append((wanted, copy))
            pl.when(wanted)(copy.start)
    for wanted, copy in copies:
        pl.when(wanted)(copy.wait)


def spread(info_ref, place_ref, sources, index, target_ref, first_column):
    last = target_ref.shape[1] // BS - 1
    count = ROWS // len(sources)
    for row in range(ROWS):
        held = local_row(info_ref, row)
        for slot in range(SLOTS):
            where = jnp.minimum(place_ref[(index + row) * SLOTS + slot] - first_column, last)
            value = sources[0][held % count, slot]
            for i in range(1, len(sources)):
                value = jnp.where(held >= i * count, sources[i][held % count, slot], value)
            target_ref[block(row), lanes(where)] = value


class Part:
    def __init__(self, ref, first):
        self.ref, self.first = ref, first

    def __getitem__(self, at):
        return self.ref[self.first + at]


def tables(ref):
    firsts = (0, 2, 2 + WINDOW * SLOTS, 2 + WINDOW * SLOTS + ROWS * WINDOW)
    return [Part(ref, first) for first in firsts]


def kept(value, mask_ref, row_pair, column_pair):
    parts = []
    for down in range(2):
        across = []
        for right in range(2):
            one = value[down * BS:(down + 1) * BS, right * BS:(right + 1) * BS]
            there = mask_ref[(2 * row_pair + down) * WINDOW + 2 * column_pair + right] > 0
            across.append(jnp.where(there, one, jnp.zeros_like(one)))
        parts.append(jnp.concatenate(across, axis=1))
    return jnp.concatenate(parts, axis=0)


class Dense:
    def __init__(self, ref, first_row, first_column):
        self.ref, self.first_row, self.first_column = ref, first_row, first_column

    def rows(self, row_pair, count=1):
        return pl.ds((2 * row_pair - self.first_row) * BS, count * TILE)

    def columns(self, column_pair, count=1):
        return pl.ds((2 * column_pair - self.first_column) * BS, count * TILE)

    def __getitem__(self, at):
        return self.ref[self.rows(at[0]), self.columns(at[1])]

    def __setitem__(self, at, value):
        self.ref[self.rows(at[0]), self.columns(at[1])] = value


class Packed:
    def __init__(self, ref, first_row, first_column):
        self.ref, self.first_row, self.first_column = ref, first_row, first_column

    def __getitem__(self, at):
        parts = []
        for row in (2 * at[0] - self.first_row, 2 * at[0] + 1 - self.first_row):
            columns = [2 * at[1] + right - self.first_column for right in range(2)]
            parts.append(jnp.concatenate(
                [self.ref[start_of(row) + c] if c < row + 5 else jnp.zeros((BS, BS), jnp.bfloat16) for c in columns], axis=1
            ))
        return jnp.concatenate(parts, axis=0)


def product(left, right, row_pair, column_pair, ks):
    ks = [k for k in sorted(ks) if abs(k - row_pair) <= 2 and abs(k - column_pair) <= 2]
    total = None
    while ks:
        source = right[ks[0]]
        count = 1
        while count < len(ks) and ks[count] == ks[0] + count and right[ks[count]].ref is source.ref:
            count += 1
        part = jnp.dot(
            left.ref[left.rows(row_pair), left.columns(ks[0], count)],
            jnp.concatenate([source[k, column_pair] for k in ks[:count]], axis=0) if isinstance(source, Packed)
            else source.ref[source.rows(ks[0], count), source.columns(column_pair)],
            preferred_element_type=jnp.float32,
        )
        total = part if total is None else total + part
        ks = ks[count:]
    return total


class Step:
    def __init__(self, pairs, low, high, early, late, wanted):
        self.pairs, self.low, self.high, self.early, self.late, self.wanted = pairs, low, high, early, late, wanted

    def columns(self, row_pair):
        return range(max(row_pair - 2, self.low), min(row_pair + 2, self.high) + 1)

    def whole(self, row_pair, column_pair):
        return not any(abs(k - row_pair) <= 2 and abs(k - column_pair) <= 2 for k in self.late)

    def places(self):
        return [(p, c) for p in self.pairs for c in self.columns(p)]

    def reached(self, row_pair, column_pair):
        return any(abs(k - row_pair) <= 2 and abs(k - column_pair) <= 2 for k in self.early)

    def open(self):
        squares = [(p, c) for p, c in self.places() if not self.whole(p, c) and self.reached(p, c)]
        cubes = [(p, c) for p in self.pairs for c in self.wanted(p) if self.done(p, c)]
        return {at: i for i, at in enumerate(squares)}, {at: i for i, at in enumerate(cubes)}

    def done(self, row_pair, column_pair):
        return [k for k in self.columns(row_pair) if self.whole(row_pair, k) and abs(k - column_pair) <= 2]

    def first(self, left, right, square, mask_ref, square_part, cube_part, begun=None):
        squares, cubes = self.open()
        for i, (p, c) in enumerate(self.places()):
            if not self.reached(p, c):
                continue
            value = product(left, right, p, c, self.early)
            if begun is not None:
                value = begun[i] + value
            if (p, c) in squares:
                square_part[squares[p, c]] = value
            else:
                square[p, c] = kept(value, mask_ref, p, c).astype(jnp.bfloat16)
        for (p, c), i in cubes.items():
            cube_part[i] = product(square, right, p, c, self.done(p, c))

    def second(self, left, right, square, ready, mask_ref, square_part, cube_part, write, begun=None):
        squares, cubes = self.open()
        late = [(p, c) for p, c in self.places() if not self.whole(p, c)]
        for i, (p, c) in enumerate(self.places()):
            if (p, c) in late:
                part = square_part[squares[p, c]] if (p, c) in squares else begun[i]
                value = part + product(left, right, p, c, self.late)
                square[p, c] = kept(value, mask_ref, p, c).astype(jnp.bfloat16)
        for p in self.pairs:
            for c in self.wanted(p):
                rest = [k for k in self.columns(p) if not self.whole(p, k)]
                cube = product(square, right, p, c, rest)
                if (p, c) in cubes:
                    cube = cube_part[cubes[p, c]] if cube is None else cube_part[cubes[p, c]] + cube
                own = (square if (p, c) in late else ready)[p, c].astype(jnp.float32)
                write(p, c, (3.0 * own - 2.0 * kept(cube, mask_ref, p, c)).astype(jnp.bfloat16))

    def all(self, left, right, square, mask_ref, write):
        for p in self.pairs:
            for c in self.columns(p):
                value = product(left, right, p, c, self.early)
                square[p, c] = kept(value, mask_ref, p, c).astype(jnp.bfloat16)
        for p in self.pairs:
            for c in self.wanted(p):
                cube = product(square, right, p, c, self.early)
                own = square[p, c].astype(jnp.float32)
                write(p, c, (3.0 * own - 2.0 * kept(cube, mask_ref, p, c)).astype(jnp.bfloat16))


OWN = Step((4, 5), 2, 7, (2, 3, 4, 5, 6, 7), (), lambda p: range(p - 2, p + 3))
LOW = Step((2, 3), 0, 5, (2, 3, 4, 5), (0, 1), lambda p: range(2, p + 3))
LAST = Step((4, 5), 2, 7, (2, 3), (6, 7), lambda p: range(p - 2, p + 3))


def own_rows_kernel(table_ref, tiles_ref, own_ref):
    info_ref, place_ref, _, _ = tables(table_ref)
    own_ref[...] = jnp.zeros_like(own_ref)
    spread(info_ref, place_ref, (tiles_ref,), 8, own_ref, 4)


def low_first_kernel(table_ref, near_ref, own_ref, low_ref, square_ref, square_part, cube_part):
    info_ref, place_ref, _, mask_ref = tables(table_ref)
    low_ref[...] = jnp.zeros_like(low_ref)
    spread(info_ref, place_ref, (near_ref,), 4, low_ref, 0)
    low, own = Dense(low_ref, 4, 0), Dense(own_ref, 8, 4)
    LOW.first(low, {2: low, 3: low, 4: own, 5: own}, Dense(square_ref, 4, 8), mask_ref, square_part, cube_part)


def own_kernel(table_ref, low_ref, own_ref, other0_ref, other1_ref, next_ref, begun_ref, high_ref, square_ref):
    info_ref, place_ref, _, mask_ref = tables(table_ref)
    high_ref[...] = jnp.zeros_like(high_ref)
    spread(info_ref, place_ref, (other0_ref, other1_ref), 12, high_ref, 8)
    low, own, high = Dense(low_ref, 4, 0), Dense(own_ref, 8, 4), Dense(high_ref, 12, 8)
    result = Dense(next_ref, 8, 4)
    next_ref[tile(4, 8), tile(7, 4)] = jnp.zeros((TILE, TILE), jnp.bfloat16)
    next_ref[tile(5, 8), tile(2, 4)] = jnp.zeros((TILE, TILE), jnp.bfloat16)

    def write(p, c, value):
        result[p, c] = value

    OWN.all(own, {2: low, 3: low, 4: own, 5: own, 6: high, 7: high}, Dense(square_ref, 8, 4), mask_ref, write)
    for i, (p, c) in enumerate(LAST.places()):
        begun_ref[i] = product(result, {4: result, 5: result}, p, c, (4, 5))


def low_second_kernel(table_ref, far_ref, low_ref, ready_ref, square_part, cube_part, sent_ref, square_ref):
    mask_ref = tables(table_ref)[3]
    low, far = Dense(low_ref, 4, 0), Packed(far_ref, 0, 0)

    def write(p, c, value):
        for down in range(2):
            for right in range(2):
                row, column = 2 * p + down - 4, 2 * c + right - 4
                if column < row + 5:
                    sent_ref[start_of(row) + column] = value[down * BS:(down + 1) * BS, right * BS:(right + 1) * BS]

    LOW.second(
        low, {0: far, 1: far, 2: low, 3: low}, Dense(square_ref, 4, 0), Dense(ready_ref, 4, 8), mask_ref,
        square_part, cube_part, write,
    )


def last_first_kernel(table_ref, sent_ref, own_ref, begun_ref, square_ref, square_part, cube_part, low_ref):
    _, _, _, mask_ref = tables(table_ref)
    for row in range(ROWS):
        for column in range(8):
            if column < row + 5:
                low_ref[block(row), block(column)] = sent_ref[start_of(row) + column]
            else:
                low_ref[block(row), block(column)] = jnp.zeros((BS, BS), jnp.bfloat16)
    low, own = Dense(low_ref, 4, 4), Dense(own_ref, 8, 4)
    LAST.first(own, {2: low, 3: low, 4: own, 5: own}, Dense(square_ref, 8, 4), mask_ref, square_part, cube_part, begun_ref)


def last_second_kernel(table_ref, own_ref, begun_ref, other_ref, ready_ref, square_part, cube_part,
                       out_ref, high_ref, square_ref, dense_ref, empty_ref, sem):
    info_ref, place_ref, slot_ref, mask_ref = tables(table_ref)
    for row in range(ROWS):
        for column in range(8):
            if column < row + 5:
                high_ref[block(3 - row), block(7 - column)] = other_ref[start_of(row) + column]
            else:
                high_ref[block(3 - row), block(7 - column)] = jnp.zeros((BS, BS), jnp.bfloat16)
    own, high = Dense(own_ref, 8, 4), Dense(high_ref, 12, 8)
    result = Dense(dense_ref, 8, 4)
    empty_ref[...] = jnp.zeros_like(empty_ref)
    for row in range(ROWS):
        for slot in range(SLOTS):
            copy = pltpu.make_async_copy(empty_ref, out_ref.at[local_row(info_ref, row), slot], sem)
            pl.when(place_ref[(8 + row) * SLOTS + slot] >= WINDOW)(copy.start)

    def write(p, c, value):
        result[p, c] = value
        for down in range(2):
            for right in range(2):
                row, column = 2 * p + down, 2 * c + right
                if abs(row - column) > HALF:
                    continue
                slot = slot_ref[(row - 8) * WINDOW + column]
                copy = pltpu.make_async_copy(
                    dense_ref.at[block(row, 8), block(column, 4)],
                    out_ref.at[local_row(info_ref, row - 8), jnp.minimum(slot, SLOTS - 1)], sem,
                )
                pl.when(slot < SLOTS)(copy.start)

    LAST.second(
        own, {4: own, 5: own, 6: high, 7: high}, Dense(square_ref, 8, 4), Dense(ready_ref, 8, 4), mask_ref,
        square_part, cube_part, write, begun_ref,
    )
    pltpu.make_async_copy(out_ref, out_ref, sem).wait()


def call(kernel, scalars, operands, outs, scratch, name, space=pltpu.VMEM, limit=12, out_space=pltpu.VMEM):
    smem, vmem = pl.BlockSpec(memory_space=pltpu.SMEM), pl.BlockSpec(memory_space=pltpu.VMEM)
    return pl.pallas_call(
        kernel,
        out_shape=outs,
        in_specs=[smem] * len(scalars) + [pl.BlockSpec(memory_space=space)] * len(operands),
        out_specs=[pl.BlockSpec(memory_space=out_space)] * len(outs),
        scratch_shapes=scratch,
        compiler_params=pltpu.CompilerParams(vmem_limit_bytes=limit * 2**20),
        cost_estimate=pl.CostEstimate(flops=0, bytes_accessed=0, transcendentals=0),
        name=name,
    )(*scalars, *operands)


def dense(columns, rows=ROWS):
    return jax.ShapeDtypeStruct((rows * BS, columns * BS), jnp.bfloat16)


def partial_sums(step):
    return [jax.ShapeDtypeStruct((len(part), TILE, TILE), jnp.float32) for part in step.open()]


def scratch(columns, rows=ROWS):
    return pltpu.VMEM((rows * BS, columns * BS), jnp.bfloat16)


def per_device(cols, tiles):
    devices = lax.axis_size("dev")
    total = cols.shape[0]
    layer = lax.axis_index("layer")
    base = lax.axis_index("dev") * ROWS + layer * (ROWS - 1)
    sign = 1 - 2 * layer
    info = jnp.stack([base, sign]).astype(jnp.int32)
    axes = ("dev", "layer")

    def shifted(value, step):
        pairs = []
        for i in range(devices):
            pairs.append((2 * i, (i + step) % devices * 2))
            pairs.append((2 * i + 1, (i - step) % devices * 2 + 1))
        return lax.ppermute(value, axes, pairs)

    def swapped(value):
        return lax.ppermute(value, "layer", [(0, 1), (1, 0)])

    near = shifted(tiles, 1)
    packed = jax.ShapeDtypeStruct((PACKED, BS, BS), jnp.bfloat16)
    (packed_rows,) = call(
        pack_kernel, (info,), (cols.T, tiles), [packed],
        [pltpu.SMEM(cols.T.shape, jnp.int32), pltpu.SemaphoreType.DMA], "pack", pltpu.HBM, 56,
    )
    far = shifted(packed_rows, 2)
    rows = (base + sign * (jnp.arange(WINDOW, dtype=jnp.int32) - FAR) + total) % total
    window = jnp.take(cols, rows, axis=0)
    where = (sign * (window - base) + FAR + 2 * total) % total
    where = jnp.where((window < total) & (where < WINDOW), where, WINDOW)
    place = where.reshape(-1)
    match = where[FAR:FAR + ROWS, :, None] == jnp.arange(WINDOW, dtype=jnp.int32)
    slot = jnp.min(jnp.where(match, jnp.arange(SLOTS, dtype=jnp.int32)[None, :, None], SLOTS), axis=1).reshape(-1)
    pattern = jnp.any(where[:, :, None] == jnp.arange(WINDOW, dtype=jnp.int32), axis=1)
    mask = pattern.astype(jnp.int32).reshape(-1)
    table = jnp.concatenate([info, place, slot, mask])

    (own,) = call(own_rows_kernel, (table,), (tiles,), [dense(13)], [], "own_rows")

    near, packed_rows, own = lax.optimization_barrier((near, packed_rows, own))
    other = [swapped(near[:2]), swapped(near[2:])]
    low, ready, *parts = call(
        low_first_kernel, (table,), (near, own), [dense(13), dense(4), *partial_sums(LOW)], [], "low_first"
    )
    begun = jax.ShapeDtypeStruct((len(LAST.places()), TILE, TILE), jnp.float32)
    current, begun = call(
        own_kernel, (table,), (low, own, *other), [dense(12), begun], [scratch(9), scratch(12)], "own"
    )
    low, current = lax.optimization_barrier((low, current))
    (sent,) = call(
        low_second_kernel, (table,), (far, low, ready, *parts), [packed], [scratch(12)], "low_second"
    )
    current_other = swapped(sent)
    ready, *parts = call(
        last_first_kernel, (table,), (sent, current, begun), [dense(4), *partial_sums(LAST)], [scratch(8)], "last_first"
    )
    (out,) = call(
        last_second_kernel, (table,), (current, begun, current_other, ready, *parts),
        [jax.ShapeDtypeStruct(tiles.shape, tiles.dtype)], [scratch(8), scratch(12), scratch(12), pltpu.VMEM((BS, BS), jnp.bfloat16), pltpu.SemaphoreType.DMA],
        "last_second", out_space=pltpu.HBM,
    )
    return out


def solution(mesh):
    return jax.shard_map(
        per_device,
        mesh=mesh,
        in_specs=(P("grp", None), P(("grp", "dev"), None, None, None)),
        out_specs=P(("grp", "dev"), None, None, None),
        check_vma=False,
    )
```

```python
import functools

import jax
import jax.numpy as jnp
from jax import lax
from jax.experimental import pallas as pl
from jax.experimental.pallas import tpu as pltpu
from jax.sharding import PartitionSpec as P

BS = 128
ROWS = 4
HALF = 4
FAR = 8
WINDOW = 16
TILE = 2 * BS


def start_of(row):
    return 5 * row + row * (row - 1) // 2


PACKED = start_of(ROWS)
SLOTS = 2 * HALF


def block(index, first=0):
    return pl.ds((index - first) * BS, BS)


def lanes(index, first=0):
    return pl.ds(pl.multiple_of((index - first) * BS, BS), BS)


def tile(index, first=0):
    return pl.ds((2 * index - first) * BS, TILE)


def local_row(info_ref, row):
    return jnp.where(info_ref[1] > 0, row, ROWS - 1 - row)


def pack_kernel(info_ref, cols_ref, tiles_ref, out_ref, table_ref, sem):
    total = cols_ref.shape[1]
    table = pltpu.make_async_copy(cols_ref, table_ref, sem)
    table.start()
    out_ref[...] = jnp.zeros_like(out_ref)
    table.wait()
    base, sign = info_ref[0], info_ref[1]
    copies = []
    for row in range(ROWS):
        held = local_row(info_ref, row)
        for slot in range(SLOTS):
            column = table_ref[slot, base + sign * row]
            where = lax.rem(sign * (column - base) + total, total)
            wanted = (column < total) & (where < HALF + ROWS)
            target = jnp.where(wanted, start_of(row) + where, 0)
            copy = pltpu.make_async_copy(tiles_ref.at[held, slot], out_ref.at[target], sem)
            copies.append((wanted, copy))
            pl.when(wanted)(copy.start)
    for wanted, copy in copies:
        pl.when(wanted)(copy.wait)


def spread(info_ref, place_ref, sources, index, target_ref, first_column):
    last = target_ref.shape[1] // BS - 1
    count = ROWS // len(sources)
    for row in range(ROWS):
        held = local_row(info_ref, row)
        for slot in range(SLOTS):
            where = jnp.minimum(place_ref[(index + row) * SLOTS + slot] - first_column, last)
            value = sources[0][held % count, slot]
            for i in range(1, len(sources)):
                value = jnp.where(held >= i * count, sources[i][held % count, slot], value)
            target_ref[block(row), lanes(where)] = value


class Part:
    def __init__(self, ref, first):
        self.ref, self.first = ref, first

    def __getitem__(self, at):
        return self.ref[self.first + at]


def tables(ref):
    firsts = (0, 2, 2 + WINDOW * SLOTS, 2 + WINDOW * SLOTS + ROWS * WINDOW)
    return [Part(ref, first) for first in firsts]


def kept(value, mask_ref, row_pair, column_pair):
    parts = []
    for down in range(2):
        across = []
        for right in range(2):
            one = value[down * BS:(down + 1) * BS, right * BS:(right + 1) * BS]
            there = mask_ref[(2 * row_pair + down) * WINDOW + 2 * column_pair + right] > 0
            across.append(jnp.where(there, one, jnp.zeros_like(one)))
        parts.append(jnp.concatenate(across, axis=1))
    return jnp.concatenate(parts, axis=0)


class Dense:
    def __init__(self, ref, first_row, first_column):
        self.ref, self.first_row, self.first_column = ref, first_row, first_column

    def rows(self, row_pair, count=1):
        return pl.ds((2 * row_pair - self.first_row) * BS, count * TILE)

    def columns(self, column_pair, count=1):
        return pl.ds((2 * column_pair - self.first_column) * BS, count * TILE)

    def __getitem__(self, at):
        return self.ref[self.rows(at[0]), self.columns(at[1])]

    def __setitem__(self, at, value):
        self.ref[self.rows(at[0]), self.columns(at[1])] = value


class Packed:
    def __init__(self, ref, first_row, first_column):
        self.ref, self.first_row, self.first_column = ref, first_row, first_column

    def __getitem__(self, at):
        parts = []
        for row in (2 * at[0] - self.first_row, 2 * at[0] + 1 - self.first_row):
            columns = [2 * at[1] + right - self.first_column for right in range(2)]
            parts.append(jnp.concatenate(
                [self.ref[start_of(row) + c] if c < row + 5 else jnp.zeros((BS, BS), jnp.bfloat16) for c in columns], axis=1
            ))
        return jnp.concatenate(parts, axis=0)


def product(left, right, row_pair, column_pair, ks):
    ks = [k for k in sorted(ks) if abs(k - row_pair) <= 2 and abs(k - column_pair) <= 2]
    total = None
    while ks:
        source = right[ks[0]]
        count = 1
        while count < len(ks) and ks[count] == ks[0] + count and right[ks[count]].ref is source.ref:
            count += 1
        part = jnp.dot(
            left.ref[left.rows(row_pair), left.columns(ks[0], count)],
            jnp.concatenate([source[k, column_pair] for k in ks[:count]], axis=0) if isinstance(source, Packed)
            else source.ref[source.rows(ks[0], count), source.columns(column_pair)],
            preferred_element_type=jnp.float32,
        )
        total = part if total is None else total + part
        ks = ks[count:]
    return total


class Step:
    def __init__(self, pairs, low, high, early, late, wanted):
        self.pairs, self.low, self.high, self.early, self.late, self.wanted = pairs, low, high, early, late, wanted

    def columns(self, row_pair):
        return range(max(row_pair - 2, self.low), min(row_pair + 2, self.high) + 1)

    def whole(self, row_pair, column_pair):
        return not any(abs(k - row_pair) <= 2 and abs(k - column_pair) <= 2 for k in self.late)

    def places(self):
        return [(p, c) for p in self.pairs for c in self.columns(p)]

    def reached(self, row_pair, column_pair):
        return any(abs(k - row_pair) <= 2 and abs(k - column_pair) <= 2 for k in self.early)

    def open(self):
        squares = [(p, c) for p, c in self.places() if not self.whole(p, c) and self.reached(p, c)]
        cubes = [(p, c) for p in self.pairs for c in self.wanted(p) if self.done(p, c)]
        return {at: i for i, at in enumerate(squares)}, {at: i for i, at in enumerate(cubes)}

    def done(self, row_pair, column_pair):
        return [k for k in self.columns(row_pair) if self.whole(row_pair, k) and abs(k - column_pair) <= 2]

    def first(self, left, right, square, mask_ref, square_part, cube_part, begun=None):
        squares, cubes = self.open()
        for i, (p, c) in enumerate(self.places()):
            if not self.reached(p, c):
                continue
            value = product(left, right, p, c, self.early)
            if begun is not None:
                value = begun[i] + value
            if (p, c) in squares:
                square_part[squares[p, c]] = value
            else:
                square[p, c] = kept(value, mask_ref, p, c).astype(jnp.bfloat16)
        for (p, c), i in cubes.items():
            cube_part[i] = product(square, right, p, c, self.done(p, c))

    def second(self, left, right, square, ready, mask_ref, square_part, cube_part, write, begun=None, masked=True):
        squares, cubes = self.open()
        late = [(p, c) for p, c in self.places() if not self.whole(p, c)]
        for i, (p, c) in enumerate(self.places()):
            if (p, c) in late:
                part = square_part[squares[p, c]] if (p, c) in squares else begun[i]
                value = part + product(left, right, p, c, self.late)
                square[p, c] = kept(value, mask_ref, p, c).astype(jnp.bfloat16)
        for p in self.pairs:
            for c in self.wanted(p):
                rest = [k for k in self.columns(p) if not self.whole(p, k)]
                cube = product(square, right, p, c, rest)
                if (p, c) in cubes:
                    cube = cube_part[cubes[p, c]] if cube is None else cube_part[cubes[p, c]] + cube
                own = (square if (p, c) in late else ready)[p, c].astype(jnp.float32)
                write(p, c, (3.0 * own - 2.0 * (kept(cube, mask_ref, p, c) if masked else cube)).astype(jnp.bfloat16))

    def all(self, left, right, square, mask_ref, write):
        for p in self.pairs:
            for c in self.columns(p):
                value = product(left, right, p, c, self.early)
                square[p, c] = kept(value, mask_ref, p, c).astype(jnp.bfloat16)
        for p in self.pairs:
            for c in self.wanted(p):
                cube = product(square, right, p, c, self.early)
                own = square[p, c].astype(jnp.float32)
                write(p, c, (3.0 * own - 2.0 * kept(cube, mask_ref, p, c)).astype(jnp.bfloat16))


OWN = Step((4, 5), 2, 7, (2, 3, 4, 5, 6, 7), (), lambda p: range(p - 2, p + 3))
LOW = Step((2, 3), 0, 5, (2, 3, 4, 5), (0, 1), lambda p: range(2, p + 3))
LAST = Step((4, 5), 2, 7, (2, 3), (6, 7), lambda p: range(p - 2, p + 3))


def own_rows_kernel(table_ref, tiles_ref, own_ref):
    info_ref, place_ref, _, _ = tables(table_ref)
    own_ref[...] = jnp.zeros_like(own_ref)
    spread(info_ref, place_ref, (tiles_ref,), 8, own_ref, 4)


def low_first_kernel(table_ref, near_ref, own_ref, low_ref, square_ref, square_part, cube_part):
    info_ref, place_ref, _, mask_ref = tables(table_ref)
    low_ref[...] = jnp.zeros_like(low_ref)
    spread(info_ref, place_ref, (near_ref,), 4, low_ref, 0)
    low, own = Dense(low_ref, 4, 0), Dense(own_ref, 8, 4)
    LOW.first(low, {2: low, 3: low, 4: own, 5: own}, Dense(square_ref, 4, 8), mask_ref, square_part, cube_part)


def own_kernel(table_ref, low_ref, own_ref, other0_ref, other1_ref, next_ref, begun_ref, high_ref, square_ref):
    info_ref, place_ref, _, mask_ref = tables(table_ref)
    high_ref[...] = jnp.zeros_like(high_ref)
    spread(info_ref, place_ref, (other0_ref, other1_ref), 12, high_ref, 8)
    low, own, high = Dense(low_ref, 4, 0), Dense(own_ref, 8, 4), Dense(high_ref, 12, 8)
    result = Dense(next_ref, 8, 4)
    next_ref[tile(4, 8), tile(7, 4)] = jnp.zeros((TILE, TILE), jnp.bfloat16)
    next_ref[tile(5, 8), tile(2, 4)] = jnp.zeros((TILE, TILE), jnp.bfloat16)

    def write(p, c, value):
        result[p, c] = value

    OWN.all(own, {2: low, 3: low, 4: own, 5: own, 6: high, 7: high}, Dense(square_ref, 8, 4), mask_ref, write)
    for i, (p, c) in enumerate(LAST.places()):
        begun_ref[i] = product(result, {4: result, 5: result}, p, c, (4, 5))


def low_second_kernel(table_ref, far_ref, low_ref, ready_ref, square_part, cube_part, sent_ref, square_ref):
    mask_ref = tables(table_ref)[3]
    low, far = Dense(low_ref, 4, 0), Packed(far_ref, 0, 0)

    def write(p, c, value):
        for down in range(2):
            for right in range(2):
                row, column = 2 * p + down - 4, 2 * c + right - 4
                if column < row + 5:
                    sent_ref[start_of(row) + column] = value[down * BS:(down + 1) * BS, right * BS:(right + 1) * BS]

    LOW.second(
        low, {0: far, 1: far, 2: low, 3: low}, Dense(square_ref, 4, 0), Dense(ready_ref, 4, 8), mask_ref,
        square_part, cube_part, write,
    )


def last_first_kernel(table_ref, sent_ref, own_ref, begun_ref, square_ref, square_part, cube_part, low_ref):
    _, _, _, mask_ref = tables(table_ref)
    for row in range(ROWS):
        for column in range(8):
            if column < row + 5:
                low_ref[block(row), block(column)] = sent_ref[start_of(row) + column]
            else:
                low_ref[block(row), block(column)] = jnp.zeros((BS, BS), jnp.bfloat16)
    low, own = Dense(low_ref, 4, 4), Dense(own_ref, 8, 4)
    LAST.first(own, {2: low, 3: low, 4: own, 5: own}, Dense(square_ref, 8, 4), mask_ref, square_part, cube_part, begun_ref)


def last_second_kernel(table_ref, own_ref, begun_ref, other_ref, ready_ref, square_part, cube_part,
                       out_ref, high_ref, square_ref, dense_ref, empty_ref, sem):
    info_ref, place_ref, slot_ref, mask_ref = tables(table_ref)
    for row in range(ROWS):
        for column in range(8):
            if column < row + 5:
                high_ref[block(3 - row), block(7 - column)] = other_ref[start_of(row) + column]
            else:
                high_ref[block(3 - row), block(7 - column)] = jnp.zeros((BS, BS), jnp.bfloat16)
    own, high = Dense(own_ref, 8, 4), Dense(high_ref, 12, 8)
    result = Dense(dense_ref, 8, 4)
    empty_ref[...] = jnp.zeros_like(empty_ref)
    for row in range(ROWS):
        for slot in range(SLOTS):
            copy = pltpu.make_async_copy(empty_ref, out_ref.at[local_row(info_ref, row), slot], sem)
            pl.when(place_ref[(8 + row) * SLOTS + slot] >= WINDOW)(copy.start)

    def write(p, c, value):
        result[p, c] = value
        for down in range(2):
            for right in range(2):
                row, column = 2 * p + down, 2 * c + right
                if abs(row - column) > HALF:
                    continue
                slot = slot_ref[(row - 8) * WINDOW + column]
                copy = pltpu.make_async_copy(
                    dense_ref.at[block(row, 8), block(column, 4)],
                    out_ref.at[local_row(info_ref, row - 8), jnp.minimum(slot, SLOTS - 1)], sem,
                )
                pl.when(slot < SLOTS)(copy.start)

    LAST.second(
        own, {4: own, 5: own, 6: high, 7: high}, Dense(square_ref, 8, 4), Dense(ready_ref, 8, 4), mask_ref,
        square_part, cube_part, write, begun_ref, masked=False,
    )
    pltpu.make_async_copy(out_ref, out_ref, sem).wait()


def call(kernel, scalars, operands, outs, scratch, name, space=pltpu.VMEM, limit=12, out_space=pltpu.VMEM):
    smem, vmem = pl.BlockSpec(memory_space=pltpu.SMEM), pl.BlockSpec(memory_space=pltpu.VMEM)
    return pl.pallas_call(
        kernel,
        out_shape=outs,
        in_specs=[smem] * len(scalars) + [pl.BlockSpec(memory_space=space)] * len(operands),
        out_specs=[pl.BlockSpec(memory_space=out_space)] * len(outs),
        scratch_shapes=scratch,
        compiler_params=pltpu.CompilerParams(vmem_limit_bytes=limit * 2**20),
        cost_estimate=pl.CostEstimate(flops=0, bytes_accessed=0, transcendentals=0),
        name=name,
    )(*scalars, *operands)


def dense(columns, rows=ROWS):
    return jax.ShapeDtypeStruct((rows * BS, columns * BS), jnp.bfloat16)


def partial_sums(step):
    return [jax.ShapeDtypeStruct((len(part), TILE, TILE), jnp.float32) for part in step.open()]


def scratch(columns, rows=ROWS):
    return pltpu.VMEM((rows * BS, columns * BS), jnp.bfloat16)


def per_device(cols, tiles):
    devices = lax.axis_size("dev")
    total = cols.shape[0]
    layer = lax.axis_index("layer")
    base = lax.axis_index("dev") * ROWS + layer * (ROWS - 1)
    sign = 1 - 2 * layer
    info = jnp.stack([base, sign]).astype(jnp.int32)
    axes = ("dev", "layer")

    def shifted(value, step):
        pairs = []
        for i in range(devices):
            pairs.append((2 * i, (i + step) % devices * 2))
            pairs.append((2 * i + 1, (i - step) % devices * 2 + 1))
        return lax.ppermute(value, axes, pairs)

    def swapped(value):
        return lax.ppermute(value, "layer", [(0, 1), (1, 0)])

    near = shifted(tiles, 1)
    packed = jax.ShapeDtypeStruct((PACKED, BS, BS), jnp.bfloat16)
    (packed_rows,) = call(
        pack_kernel, (info,), (cols.T, tiles), [packed],
        [pltpu.SMEM(cols.T.shape, jnp.int32), pltpu.SemaphoreType.DMA], "pack", pltpu.HBM, 56,
    )
    far = shifted(packed_rows, 2)
    rows = (base + sign * (jnp.arange(WINDOW, dtype=jnp.int32) - FAR) + total) % total
    window = jnp.take(cols, rows, axis=0)
    where = (sign * (window - base) + FAR + 2 * total) % total
    where = jnp.where((window < total) & (where < WINDOW), where, WINDOW)
    place = where.reshape(-1)
    match = where[FAR:FAR + ROWS, :, None] == jnp.arange(WINDOW, dtype=jnp.int32)
    slot = jnp.min(jnp.where(match, jnp.arange(SLOTS, dtype=jnp.int32)[None, :, None], SLOTS), axis=1).reshape(-1)
    pattern = jnp.any(where[:, :, None] == jnp.arange(WINDOW, dtype=jnp.int32), axis=1)
    mask = pattern.astype(jnp.int32).reshape(-1)
    table = jnp.concatenate([info, place, slot, mask])

    (own,) = call(own_rows_kernel, (table,), (tiles,), [dense(13)], [], "own_rows")

    near, packed_rows, own = lax.optimization_barrier((near, packed_rows, own))
    other = [swapped(near[:2]), swapped(near[2:])]
    low, ready, *parts = call(
        low_first_kernel, (table,), (near, own), [dense(13), dense(4), *partial_sums(LOW)], [], "low_first"
    )
    begun = jax.ShapeDtypeStruct((len(LAST.places()), TILE, TILE), jnp.float32)
    current, begun = call(
        own_kernel, (table,), (low, own, *other), [dense(12), begun], [scratch(9), scratch(12)], "own"
    )
    low, current = lax.optimization_barrier((low, current))
    (sent,) = call(
        low_second_kernel, (table,), (far, low, ready, *parts), [packed], [scratch(12)], "low_second"
    )
    current_other = swapped(sent)
    ready, *parts = call(
        last_first_kernel, (table,), (sent, current, begun), [dense(4), *partial_sums(LAST)], [scratch(8)], "last_first"
    )
    (out,) = call(
        last_second_kernel, (table,), (current, begun, current_other, ready, *parts),
        [jax.ShapeDtypeStruct(tiles.shape, tiles.dtype)], [scratch(8), scratch(12), scratch(12), pltpu.VMEM((BS, BS), jnp.bfloat16), pltpu.SemaphoreType.DMA],
        "last_second", out_space=pltpu.HBM,
    )
    return out


def solution(mesh):
    return jax.shard_map(
        per_device,
        mesh=mesh,
        in_specs=(P("grp", None), P(("grp", "dev"), None, None, None)),
        out_specs=P(("grp", "dev"), None, None, None),
        check_vma=False,
    )
```
